32 devices in a mesh: expert: 4 (over x, core), tensor: 8 (over z, y).
Axes of the slice: x: 2, y: 2, z: 4, core: 2. Of those that a mesh axis runs over, the one named last changes fastest.
Arguments:
- tokens: bfloat16 [8192, 2048], P(('expert', 'tensor')), may hold values from -6 to 6
- segments: int32 [8, 1024], P('expert'), may hold values from 0 to 3, never falling along the last dimension, each value on 1 to 512 neighbouring positions
- routes: int32 [8192, 8], P(('expert', 'tensor')), may hold values from 0 to 15, all different within a row; in each aligned block of 256 rows (0 to 255, 256 to 511, ...) at most 256 rows name the same one
- norm_gain: float32 [2048], replicated, may hold values from 0.5 to 1.5
- w_query: bfloat16 [2048, 2048], P('expert', 'tensor'), may hold values from -0.125 to 0.125
- w_key: bfloat16 [2048, 2048], P('expert', 'tensor'), may hold values from -0.125 to 0.125
- w_value: bfloat16 [2048, 2048], P('expert', 'tensor'), may hold values from -0.125 to 0.125
- query_gain: float32 [128], replicated, may hold values from 0.5 to 1.5
- key_gain: float32 [128], replicated, may hold values from 0.5 to 1.5
- w_out: bfloat16 [2048, 2048], P('tensor', 'expert'), may hold values from -1 to 1
- mix_gain: float32 [2048], replicated, may hold values from 0.5 to 1.5
- w_router: bfloat16 [2048, 16], replicated, may hold values from -0.0625 to 0.0625
- w_gate: bfloat16 [32, 2048, 512], P(('expert', 'tensor')), may hold values from -0.125 to 0.125
- w_up: bfloat16 [32, 2048, 512], P(('expert', 'tensor')), may hold values from -0.125 to 0.125
- w_down: bfloat16 [32, 512, 2048], P(('expert', 'tensor')), may hold values from -0.75 to 0.75
- cotangent: bfloat16 [8192, 2048], P(('expert', 'tensor')), may hold values from -6 to 6
Outputs:
- layer_out: bfloat16 [8192, 2048], P(('expert', 'tensor'))
- grad_tokens: bfloat16 [8192, 2048], P(('expert', 'tensor'))
- grad_norm_gain: float32 [2048], replicated
- grad_w_query: float32 [2048, 2048], P('expert', 'tensor')
- grad_w_key: float32 [2048, 2048], P('expert', 'tensor')
- grad_w_value: float32 [2048, 2048], P('expert', 'tensor')
- grad_query_gain: float32 [128], replicated
- grad_key_gain: float32 [128], replicated
- grad_w_out: float32 [2048, 2048], P('tensor', 'expert')
- grad_mix_gain: float32 [2048], replicated
- grad_w_router: float32 [2048, 16], replicated
- grad_w_gate: float32 [32, 2048, 512], P(('expert', 'tensor'))
- grad_w_up: float32 [32, 2048, 512], P(('expert', 'tensor'))
- grad_w_down: float32 [32, 512, 2048], P(('expert', 'tensor'))
The draws below stay inside these ranges and needn't reach their ends.
Inputs may be any that keep to these rules, and one draw needn't show every extreme that they name: `segments`: within a sequence the numbers never fall, every document has 1 to half of 1024 tokens, and one document of each sequence has exactly half of 1024. `routes`: each token names 8 different experts; among the 256 tokens of one device no expert is named more than 256 times, and in every draw some device names some expert exactly 256 times.
All inputs are finite; a program needn't handle non-finite values.
Results may differ from the reference program's by a relative error of at most 0.025.
Values may be sent and summed in bfloat16 or wider, within the bound.
No kernel may reach another device: no remote copies, remote signals or barrier semaphores. Data moves between devices by JAX's collectives and lax.ppermute only.
A program may use at most 576 MiB of HBM per device.

```python
import math
import jax
import jax.numpy as jnp
import numpy as np
from jax import lax

D = 2048
HEADS = 16
HD = 128
FF_E = 1024
TOP = 8
WIN = 1024
LEN = 1024
DOCS = 4
EXPERTS = 16
SEQS = 8
TOKENS = 8192
TOK_DEV = 256
CAP = 256
N_EXPERT = 4
N_TENSOR = 8


def block_scale(rng, shape, shards, smallest, largest):
    level = 1.0
    for axis_at, shards_of in shards:
        heights = jax.random.uniform(jax.random.fold_in(jax.random.fold_in(rng, 6), axis_at), (shards_of,), jnp.float32, smallest / len(shards), largest / len(shards))
        level = level * jnp.repeat(jnp.exp(heights), shape[axis_at] // shards_of).reshape((-1,) + (1,) * (len(shape) - 1 - axis_at))
    return level


def split_up(number_of, total, most, skew):
    loads = [(1 << 20) // math.isqrt(rank ** skew) + 1 for rank in range(2, number_of + 1)]
    rest, given = total - most - (number_of - 1), [1] * (number_of - 1)
    while rest > 0:
        free = [i for i in range(number_of - 1) if given[i] < most]
        whole, left = sum([loads[i] for i in free]), rest
        for i in free:
            extra = min(most - given[i], max(1, left * loads[i] // whole), rest)
            given[i] = given[i] + extra
            rest = rest - extra
    return np.array([most] + given)


def ragged_sizes(key, number_of, total, most, skew):
    if number_of == 2:
        one = jax.random.randint(key, (), max(1, total - most), min(most, total - 1) + 1)
        return jnp.stack([one, total - one])
    sizes = jnp.asarray(split_up(number_of, total, most, skew), jnp.int32)
    pairs = (number_of - 1) // 2
    source_of, sink = sizes[1:1 + 2 * pairs:2], sizes[2:2 + 2 * pairs:2]
    slack = jnp.minimum(source_of - 1, most - sink)
    moved = jax.random.randint(jax.random.fold_in(key, 1), (pairs,), 0, 1 << 20) % (slack + 1)
    sizes = sizes.at[1:1 + 2 * pairs:2].set(source_of - moved).at[2:2 + 2 * pairs:2].set(sink + moved)
    return sizes[jax.random.permutation(jax.random.fold_in(key, 2), number_of)]


def deal_out(key, own, number, rows, number_of, top, limit, slope):
    order = jax.random.permutation(key, number_of)
    heavy_load, ordinary = load_shares(number_of, rows * top, limit, slope, True), load_shares(number_of, rows * top, limit, slope, False)
    places = jnp.arange(number_of)

    def named(lengths, turn):
        used = int((lengths > 0).sum())
        fixed = max(1, used // 4)
        shifted = fixed + (places - fixed + turn * (used - fixed)) % max(1, number_of - fixed)
        return jnp.zeros((number_of,), jnp.int32).at[order[jnp.where(places < fixed, places, shifted)]].set(jnp.asarray(lengths, jnp.int32))

    lengths = jnp.where(number % 4 == 0, named(heavy_load, number // 4), named(ordinary, number - number // 4 - 1))
    mixed = jax.random.permutation(jax.random.fold_in(own, 3), number_of)
    source_of, receiver = mixed[0:number_of // 2 * 2:2], mixed[1:number_of // 2 * 2:2]
    slack = jnp.minimum(lengths[source_of] - 1, limit - lengths[receiver]) // 2
    slack = jnp.where((source_of == order[0]) | (receiver == order[0]) | (lengths[receiver] == 0), 0, jnp.maximum(slack, 0))
    shifted = jax.random.randint(jax.random.fold_in(own, 4), (number_of // 2,), 0, 1 << 20) % (slack + 1)
    lengths = lengths.at[source_of].add(-shifted).at[receiver].add(shifted)
    items = jnp.searchsorted(jnp.cumsum(lengths), jnp.arange(rows * top), side="right").astype(jnp.int32)
    listing = items.reshape(top, rows).T
    listing = listing[jax.random.permutation(jax.random.fold_in(own, 1), rows)]
    turn = jax.random.randint(jax.random.fold_in(own, 2), (rows, 1), 0, top)
    return jnp.take_along_axis(listing, (jnp.arange(top)[None, :] + turn) % top, axis=1)


def load_shares(number_of, total, reach, slope, full):
    portions = [(1 << 20) // math.isqrt(grade ** slope) + 1 for grade in range(1, number_of + 1)]
    largest = reach if full else min(reach, max(-(-total // number_of), total * portions[0] // sum(portions)))
    least = 1 if total - largest >= number_of - 1 else 0
    holding, spare = [largest] + [least] * (number_of - 1), total - largest - least * (number_of - 1)
    while spare > 0:
        candidates = [i for i in range(1, number_of) if holding[i] < largest] or [i for i in range(1, number_of) if holding[i] < reach]
        whole, left = sum([portions[i] for i in candidates]), spare
        for i in candidates:
            extra = min(reach - holding[i], max(1, left * portions[i] // whole), spare)
            holding[i] = holding[i] + extra
            spare = spare - extra
    return np.array(holding)


def gaussian(key, extent, width, limit, pieces=(), kind=jnp.bfloat16):
    drawn = width * jax.random.normal(key, extent, jnp.float32)
    if pieces:
        drawn = drawn * block_scale(key, extent, pieces, -0.22, 0.18)
    return jnp.clip(drawn, -limit, limit).astype(kind)


def setup_inputs(seed: int = 0) -> dict:
    keys = jax.random.split(jax.random.key(seed), 17)
    tokens = gaussian(keys[0], (TOKENS, D), 1.0, 6.0, ((0, 32),))
    segments = jax.vmap(lambda own: jnp.searchsorted(jnp.cumsum(ragged_sizes(own, DOCS, LEN, LEN // 2, 2)), jnp.arange(LEN), side="right"))(jax.random.split(keys[1], SEQS)).reshape((SEQS, LEN)).astype(jnp.int32)
    routes_keys = jax.random.split(jax.random.fold_in(keys[2], 1), TOKENS // TOK_DEV)
    routes_turns = jax.random.permutation(jax.random.fold_in(keys[2], 3), TOKENS // TOK_DEV)
    routes = jax.vmap(lambda own, number: deal_out(jax.random.fold_in(keys[2], 2), own, number, TOK_DEV, EXPERTS, TOP, CAP, 2))(routes_keys, routes_turns).reshape((TOKENS, TOP))
    norm_gain = jnp.clip(1.0 + 0.1 * jax.random.normal(keys[3], (D,), jnp.float32), 0.5, 1.5)
    w_query = gaussian(keys[4], (D, HEADS * HD), D ** -0.5, 0.125, ((0, 4), (1, 8)))
    w_key = gaussian(keys[5], (D, HEADS * HD), D ** -0.5, 0.125, ((0, 4), (1, 8)))
    w_value = gaussian(keys[6], (D, HEADS * HD), D ** -0.5, 0.125, ((0, 4), (1, 8)))
    query_gain = jnp.clip(1.0 + 0.1 * jax.random.normal(keys[7], (HD,), jnp.float32), 0.5, 1.5)
    key_gain = jnp.clip(1.0 + 0.1 * jax.random.normal(keys[8], (HD,), jnp.float32), 0.5, 1.5)
    w_out = gaussian(keys[9], (HEADS * HD, D), (HEADS * HD // 64) ** -0.5, 1.0, ((0, 8), (1, 4)))
    mix_gain = jnp.clip(1.0 + 0.1 * jax.random.normal(keys[10], (D,), jnp.float32), 0.5, 1.5)
    w_router = gaussian(keys[11], (D, EXPERTS), (4 * D) ** -0.5, 0.0625)
    w_gate = gaussian(keys[12], (2 * EXPERTS, D, FF_E // 2), D ** -0.5, 0.125, ((0, 32),))
    w_up = gaussian(keys[13], (2 * EXPERTS, D, FF_E // 2), D ** -0.5, 0.125, ((0, 32),))
    w_down = gaussian(keys[14], (2 * EXPERTS, FF_E // 2, D), (FF_E // 16) ** -0.5, 0.75, ((0, 32),))
    cotangent = gaussian(keys[15], (TOKENS, D), 1.0, 6.0, ((0, 32),))
    return dict(tokens=tokens, segments=segments, routes=routes, norm_gain=norm_gain, w_query=w_query, w_key=w_key, w_value=w_value, query_gain=query_gain, key_gain=key_gain, w_out=w_out, mix_gain=mix_gain, w_router=w_router, w_gate=w_gate, w_up=w_up, w_down=w_down, cotangent=cotangent)


EPSILON = 1e-05
THETA = 50000.0
MASKED = -1e+30
HIGH = lax.Precision.HIGHEST

@jax.custom_vjp
def low(v):
    return lax.optimization_barrier(v.astype(jnp.bfloat16)).astype(jnp.float32)

@jax.custom_vjp
def low_back(v):
    return v

def low_keep(v):
    return (low(v), None)

def low_pass(kept, grad):
    return (grad,)

def back_keep(v):
    return (v, None)

def back_low(kept, grad):
    return (low(grad),)
low.defvjp(low_keep, low_pass)
low_back.defvjp(back_keep, back_low)

def rope_tables(length, head_size):
    half_size = head_size // 2
    frequency = THETA ** (-2.0 * jnp.arange(half_size, dtype=jnp.float32) / head_size)
    angles = jnp.arange(length, dtype=jnp.float32)[:, None] * frequency[None, :]
    return (jnp.cos(angles)[:, None, :], jnp.sin(angles)[:, None, :])

def qk_prepare(projected, gain_vec, cos_part, sin_part):
    scaled = projected * lax.rsqrt(lax.optimization_barrier(jnp.mean(projected * projected, axis=-1, keepdims=True)) + EPSILON) * gain_vec
    half_size = scaled.shape[-1] // 2
    first_half = scaled[..., :half_size]
    second = scaled[..., half_size:]
    return jnp.concatenate([first_half * cos_part - second * sin_part, second * cos_part + first_half * sin_part], axis=-1)

def allowed_pairs(seg_row):
    length = seg_row.shape[0]
    position = jnp.arange(length, dtype=jnp.int32)
    near_pairs = jnp.abs(position[:, None] - position[None, :]) < WIN
    return near_pairs & (seg_row[:, None] == seg_row[None, :])

def route_tables(routes):
    sources = N_EXPERT * N_TENSOR
    total_routes = TOKENS * TOP
    flat_expert = routes.reshape(-1).astype(jnp.int32)
    hit_table = (flat_expert[:, None] == jnp.arange(EXPERTS, dtype=jnp.int32)[None, :]).astype(jnp.int32)
    run_counts = jnp.cumsum(hit_table.reshape(sources, TOK_DEV * TOP, EXPERTS), axis=1).reshape(total_routes, EXPERTS)
    slot_of = (lax.optimization_barrier(jnp.sum(run_counts * hit_table, axis=1)) - 1).astype(jnp.int32)
    route_order = jnp.arange(total_routes, dtype=jnp.int32)
    column = (route_order // (TOK_DEV * TOP) * CAP + slot_of).astype(jnp.int32)
    table_width = sources * CAP
    token_table = jnp.zeros((EXPERTS, table_width), jnp.int32).at[flat_expert, column].set(route_order // TOP)
    route_table = jnp.zeros((EXPERTS, table_width), jnp.int32).at[flat_expert, column].set(route_order)
    valid_table = jnp.zeros((EXPERTS, table_width), jnp.float32).at[flat_expert, column].set(1.0)
    return (token_table, route_table, valid_table)

def reference(tokens, segments, routes, norm_gain, w_query, w_key, w_value, query_gain, key_gain, w_out, mix_gain, w_router, w_gate, w_up, w_down, cotangent):
    token_table, route_table, valid_table = route_tables(routes)
    cos_part, sin_part = rope_tables(LEN, HD)
    shape_heads = (SEQS, LEN, HEADS, HD)

    def forward(params):
        inputs, gain_one, query_w, key_w, value_w, query_g, key_g, out_w, gain_two, router_w, gate_w, up_w, down_w = params
        inv_one = lax.rsqrt(lax.optimization_barrier(jnp.mean(inputs * inputs, axis=-1, keepdims=True)) + EPSILON)
        normed_one = low(inputs * inv_one * gain_one)
        query_proj = low_back(jnp.dot(normed_one, query_w, precision=HIGH)).reshape(shape_heads)
        key_proj = low_back(jnp.dot(normed_one, key_w, precision=HIGH)).reshape(shape_heads)
        value_low = low_back(low(jnp.dot(normed_one, value_w, precision=HIGH))).reshape(shape_heads)
        query_low = low(qk_prepare(query_proj, query_g, cos_part, sin_part))
        key_low = low(qk_prepare(key_proj, key_g, cos_part, sin_part))

        def one_sequence(item_list):
            query_seq, key_seq, value_seq, seg_row = item_list
            scores = low_back(jnp.einsum('qhd,khd->hqk', query_seq, key_seq, precision=HIGH) * HD ** (-0.5))
            scores = jnp.where(allowed_pairs(seg_row)[None], scores, MASKED)
            prob_vals = low_back(low(jax.nn.softmax(scores, axis=-1)))
            return jnp.einsum('hqk,khd->qhd', prob_vals, value_seq, precision=HIGH)
        attended = lax.map(jax.checkpoint(one_sequence), (query_low, key_low, value_low, segments))
        attn_rows = low_back(low(attended.reshape(TOKENS, HEADS * HD)))
        branch = low_back(jnp.dot(attn_rows, out_w, precision=HIGH))
        residual = inputs + branch
        inv_two = lax.rsqrt(lax.optimization_barrier(jnp.mean(residual * residual, axis=-1, keepdims=True)) + EPSILON)
        normed_two = low(residual * inv_two * gain_two)
        logits = jnp.dot(normed_two, router_w, precision=HIGH)
        gate_weights = jax.nn.softmax(jnp.take_along_axis(logits, routes, axis=1), axis=-1)
        gate_flat = gate_weights.reshape(-1)
        gate_full = gate_w.reshape(EXPERTS, 2, D, FF_E // 2).transpose(0, 2, 1, 3).reshape(EXPERTS, D, FF_E)
        up_full = up_w.reshape(EXPERTS, 2, D, FF_E // 2).transpose(0, 2, 1, 3).reshape(EXPERTS, D, FF_E)
        down_full = down_w.reshape(EXPERTS, FF_E, D)

        def one_expert(item_list):
            token_idx, route_idx, valid_mask, gate_e, up_e, down_e = item_list
            expert_rows = low_back(normed_two[token_idx] * valid_mask[:, None])
            gate_pre = low_back(jnp.dot(expert_rows, gate_e, precision=HIGH))
            up_pre = low_back(jnp.dot(expert_rows, up_e, precision=HIGH))
            activation = low(jax.nn.silu(gate_pre) * up_pre)
            expert_out = low_back(low(jnp.dot(activation, down_e, precision=HIGH)))
            return expert_out * (gate_flat[route_idx] * valid_mask)[:, None]
        contrib = lax.map(jax.checkpoint(one_expert), (token_table, route_table, valid_table, gate_full, up_full, down_full))
        mixture = jnp.zeros((TOKENS, D), jnp.float32).at[token_table.reshape(-1)].add(contrib.reshape(-1, D))
        return residual + mixture
    params = (tokens.astype(jnp.float32), norm_gain.astype(jnp.float32), w_query.astype(jnp.float32), w_key.astype(jnp.float32), w_value.astype(jnp.float32), query_gain.astype(jnp.float32), key_gain.astype(jnp.float32), w_out.astype(jnp.float32), mix_gain.astype(jnp.float32), w_router.astype(jnp.float32), w_gate.astype(jnp.float32), w_up.astype(jnp.float32), w_down.astype(jnp.float32))
    output, pull = jax.vjp(forward, params)
    grads = pull(cotangent.astype(jnp.float32))[0]
    return (output.astype(jnp.bfloat16), grads[0].astype(jnp.bfloat16), grads[1], grads[2], grads[3], grads[4], grads[5], grads[6], grads[7], grads[8], grads[9], grads[10], grads[11], grads[12])
```

```python
import jax
import jax.numpy as jnp
from jax import lax
from jax.sharding import PartitionSpec as P

WIN = 1024


EPSILON = 1e-05
THETA = 50000.0
MASKED = -1e30
HIGH = lax.Precision.HIGHEST
LOW = jnp.bfloat16
FULL = jnp.float32


def inner_rows(left_side, right_side, precision=None):
    return lax.dot_general(
        left_side,
        right_side,
        (((0,), (0,)), ((), ())),
        precision=precision,
        preferred_element_type=jnp.float32,
    )


def outer_rows(left_side, right_side, precision=None):
    return lax.dot_general(
        left_side,
        right_side,
        (((1,), (1,)), ((), ())),
        precision=precision,
        preferred_element_type=jnp.float32,
    )


def plain_dot(left_side, right_side):
    return jnp.dot(left_side, right_side, preferred_element_type=jnp.float32)


def rope_tables(length, head_size):
    half_size = head_size // 2
    frequency = THETA ** (-2.0 * jnp.arange(half_size, dtype=jnp.float32) / head_size)
    angles = jnp.arange(length, dtype=jnp.float32)[:, None] * frequency[None, :]
    return (jnp.cos(angles), jnp.sin(angles))


def qk_prepare(projected, gain_vec, cos_part, sin_part):
    scaled = (
        projected
        * lax.rsqrt(jnp.mean(projected * projected, axis=-1, keepdims=True) + EPSILON)
        * gain_vec
    )
    half_size = scaled.shape[-1] // 2
    first_half = scaled[..., :half_size]
    second = scaled[..., half_size:]
    return jnp.concatenate(
        [first_half * cos_part - second * sin_part, second * cos_part + first_half * sin_part],
        axis=-1,
    )


def allowed_pairs(seg_row, position):
    same = seg_row[:, None] == seg_row[None, :]
    if position.shape[0] > WIN:
        same = same & (jnp.abs(position[:, None] - position[None, :]) < WIN)
    return same


def attend_item(item_list, mask):
    query_block, key_block, value_block = item_list
    scaling = query_block.shape[-1] ** (-0.5)
    scores = outer_rows(query_block, key_block) * scaling
    scores = jnp.where(mask, scores, MASKED)
    row_max = jnp.max(scores, axis=-1, keepdims=True)
    exponent = jnp.exp(scores - row_max)
    row_total = jnp.sum(exponent, axis=-1, keepdims=True)
    prob_vals = (exponent / row_total).astype(jnp.bfloat16)
    attended = jnp.dot(prob_vals, value_block, preferred_element_type=jnp.float32)
    return (attended.astype(LOW), (row_max + jnp.log(row_total))[:, 0])


def attend_back(item_list, mask):
    query_block, key_block, value_block, grad_block, log_total = item_list
    scaling = query_block.shape[-1] ** (-0.5)
    scores = outer_rows(query_block, key_block) * scaling
    prob_vals = jnp.where(mask, jnp.exp(scores - log_total[:, None]), 0.0)
    grad_prob = outer_rows(grad_block, value_block).astype(jnp.bfloat16).astype(jnp.float32)
    grad_value = inner_rows(prob_vals.astype(jnp.bfloat16), grad_block)
    centre = jnp.sum(prob_vals * grad_prob, axis=-1, keepdims=True)
    grad_score = (prob_vals * (grad_prob - centre)).astype(jnp.bfloat16)
    grad_query = jnp.dot(grad_score, key_block, preferred_element_type=jnp.float32) * scaling
    grad_key = inner_rows(grad_score, query_block) * scaling
    return (grad_query, grad_key, grad_value)


class Ring:
    def __init__(self, axis, size, count):
        self.axis, self.count = axis, count
        self.order = list(range(0, count, 2)) + list(range(count - 1, 0, -2))
        self.rightward = [
            (base + self.order[k], base + self.order[(k + 1) % count])
            for base in range(0, size, count)
            for k in range(count)
        ]
        self.leftward = [(to, start) for start, to in self.rightward]

    def right(self, value):
        return jax.tree.map(lambda v: lax.ppermute(v, self.axis, self.rightward), value)

    def left(self, value):
        return jax.tree.map(lambda v: lax.ppermute(v, self.axis, self.leftward), value)

    def members(self, place):
        order = jnp.array(self.order, jnp.int32)
        spot = jnp.argmax(order == place).astype(jnp.int32)
        shifts = [0]
        for k in range(1, self.count // 2):
            shifts += [-k, k]
        shifts.append(self.count // 2)
        return order[(spot + jnp.array(shifts, jnp.int32)) % self.count]

    def gather(self, value):
        from_left = from_right = value
        blocks = [value]
        for _ in range(1, self.count // 2):
            from_left, from_right = self.right(from_left), self.left(from_right)
            blocks += [from_left, from_right]
        upper = self.right(jax.tree.map(lambda v: v[: v.shape[0] // 2], from_left))
        lower = self.left(jax.tree.map(lambda v: v[v.shape[0] // 2 :], from_right))
        blocks.append(jax.tree.map(lambda u, v: jnp.concatenate([u, v]), upper, lower))
        return blocks

    def scatter(self, blocks):
        half = blocks[-1].shape[0] // 2
        from_left, from_right = self.right(blocks[-1][:half]), self.left(blocks[-1][half:])
        for k in range(self.count // 2 - 1, 0, -1):
            on_left, on_right = blocks[2 * k - 1], blocks[2 * k]
            if from_left.shape[0] == half:
                to_right = jnp.concatenate([on_right[:half] + from_left, on_right[half:]])
                to_left = jnp.concatenate([on_left[:half], on_left[half:] + from_right])
            else:
                to_right, to_left = on_right + from_left, on_left + from_right
            from_left, from_right = self.right(to_right), self.left(to_left)
        return blocks[0].astype(FULL) + from_left.astype(FULL) + from_right.astype(FULL)


def everywhere(value):
    for axis in ("expert", "tensor"):
        size, step = lax.axis_size(axis), 1
        while step < size:
            pairs = [(i, i ^ step) for i in range(size)]
            value = jax.tree.map(lambda v: v + lax.ppermute(v, axis, pairs), value)
            step *= 2
    return value


def expert_chunk(rows, grad_out, gates, gate_mat, up_mat, down_mat):
    gate_pre, up_pre = plain_dot(rows, gate_mat), plain_dot(rows, up_mat)
    sigmoid_val = jax.nn.sigmoid(gate_pre)
    silu_val = gate_pre * sigmoid_val
    activation = (silu_val * up_pre).astype(LOW).astype(FULL)
    plain_grad = outer_rows(grad_out, down_mat)
    grad_gates = jnp.sum(activation * plain_grad, axis=-1)
    grad_act = gates[:, None] * plain_grad
    grad_gate_pre = (
        grad_act * up_pre * sigmoid_val * (1.0 + gate_pre * (1.0 - sigmoid_val))
    ).astype(LOW)
    grad_up_pre = (grad_act * silu_val).astype(LOW)
    weighted = (gates[:, None] * activation).astype(LOW)
    grad_rows = outer_rows(grad_gate_pre, gate_mat) + outer_rows(grad_up_pre, up_mat)
    mixed = plain_dot(weighted, down_mat)
    return mixed, grad_rows, grad_gates, weighted, grad_gate_pre, grad_up_pre


def per_device(
    tokens,
    segments,
    routes,
    norm_gain,
    w_query,
    w_key,
    w_value,
    query_gain,
    key_gain,
    w_out,
    mix_gain,
    w_router,
    w_gate,
    w_up,
    w_down,
    cotangent,
):
    group_count, tensor_count = lax.axis_size("expert"), lax.axis_size("tensor")
    expert_count = w_router.shape[1]
    tok_rows, model_width = tokens.shape
    seq_count, length = segments.shape
    head_size = query_gain.shape[0]
    part_count = tensor_count // seq_count
    block_width = w_query.shape[1]
    local_width = seq_count * block_width
    heads_here = local_width // head_size
    group_at, tensor_at = lax.axis_index("expert"), lax.axis_index("tensor")
    seq_at, part_at = tensor_at // part_count, tensor_at % part_count
    whole_ring = Ring("tensor", tensor_count, tensor_count)
    seq_ring = Ring("tensor", tensor_count, part_count)

    def swap(value, axis, pairs):
        return lax.ppermute(value, axis, pairs)

    core_pairs = [(i, i ^ 1) for i in range(group_count)]

    def chip_pairs(shift):
        return [(i, (i + 2 * shift) % group_count) for i in range(group_count)]

    def seq_pairs(shift):
        return [(t, (t + part_count * shift) % tensor_count) for t in range(tensor_count)]

    def blocks_of(value, axis):
        return jnp.concatenate(
            [value] + [swap(value, "tensor", seq_pairs(s)) for s in range(1, seq_count)], axis=axis
        )

    inputs = tokens.astype(jnp.float32)
    inv_one = lax.rsqrt(jnp.mean(inputs * inputs, axis=-1, keepdims=True) + EPSILON)
    unit_one = inputs * inv_one
    normed_one = (unit_one * norm_gain).astype(jnp.bfloat16)
    query_full, key_full, value_full = (
        lax.all_gather(blocks_of(w, 1), "expert", axis=0, tiled=True)
        for w in (w_query, w_key, w_value)
    )
    out_full = lax.all_gather(blocks_of(w_out, 0), "expert", axis=1, tiled=True)
    normed_all = jnp.concatenate(seq_ring.gather(normed_one))

    members = seq_ring.members(part_at)
    cos_part, sin_part = (
        table.reshape(part_count, tok_rows, 1, head_size // 2)[members].reshape(
            length, 1, head_size // 2
        )
        for table in rope_tables(length, head_size)
    )
    seg_row = segments[seq_at].reshape(part_count, tok_rows)[members].reshape(length)
    position = (
        jnp.arange(length, dtype=jnp.int32).reshape(part_count, tok_rows)[members].reshape(length)
    )
    mask = allowed_pairs(seg_row, position)
    shape_heads = (length, heads_here, head_size)

    query_proj = plain_dot(normed_all, query_full).reshape(shape_heads)
    key_proj = plain_dot(normed_all, key_full).reshape(shape_heads)
    value_low = plain_dot(normed_all, value_full).astype(LOW).reshape(shape_heads)
    query_low = qk_prepare(query_proj, query_gain, cos_part, sin_part).astype(LOW)
    key_low = qk_prepare(key_proj, key_gain, cos_part, sin_part).astype(LOW)

    def to_items(heads_arr):
        return heads_arr.transpose(1, 0, 2)

    def from_items(item_arr):
        return item_arr.transpose(1, 0, 2)

    query_items, key_items, value_items = map(to_items, (query_low, key_low, value_low))
    attended, log_total = lax.map(
        lambda items: attend_item(items, mask), (query_items, key_items, value_items)
    )
    attn_rows = from_items(attended).reshape(length, local_width)
    partial_branch = [
        plain_dot(attn_rows[k * tok_rows : (k + 1) * tok_rows], out_full).astype(LOW)
        for k in range(part_count)
    ]
    residual = inputs + seq_ring.scatter(partial_branch)
    inv_two = lax.rsqrt(jnp.mean(residual * residual, axis=-1, keepdims=True) + EPSILON)
    unit_two = residual * inv_two
    normed_two = (unit_two * mix_gain).astype(jnp.bfloat16)
    logits = jnp.dot(normed_two, w_router, preferred_element_type=jnp.float32)
    hits = jnp.any(
        routes[:, :, None] == jnp.arange(expert_count, dtype=jnp.int32)[None, None, :], axis=1
    )
    top_logit = jnp.max(jnp.where(hits, logits, MASKED), axis=-1, keepdims=True)
    raised = jnp.where(hits, jnp.exp(logits - top_logit), 0.0)
    gate_table = raised / jnp.sum(raised, axis=-1, keepdims=True)

    grad_out = cotangent.astype(jnp.float32)
    cot_blocks = whole_ring.gather(cotangent)
    row_blocks = whole_ring.gather(normed_two)
    gate_blocks = whole_ring.gather(gate_table)
    slabs = []
    for shift in range(group_count // 2):
        mine = [
            w[0] if shift == 0 else swap(w[0], "expert", chip_pairs(shift))
            for w in (w_gate, w_up, w_down)
        ]
        theirs = [swap(w, "expert", core_pairs) for w in mine]
        for cross, mats in ((0, mine), (1, theirs)):
            chip = (group_at // 2 - shift) % (group_count // 2)
            owner = (chip * 2 + (group_at % 2 ^ cross)) * tensor_count + tensor_at
            slabs.append((mats, owner // 2))
    block_count = len(row_blocks)
    mixed_parts, grad_row_parts, grad_gate_parts = [], [], []
    kept = [[] for _ in slabs]
    for k in range(block_count):
        mixed, grad_rows, grad_table = 0.0, 0.0, 0.0
        for s, (mats, expert_at) in enumerate(slabs):
            column = jnp.arange(expert_count) == expert_at
            gates = jnp.sum(jnp.where(column[None, :], gate_blocks[k], 0.0), axis=1)
            mixed_s, rows_s, gates_s, *keep = expert_chunk(
                row_blocks[k], cot_blocks[k], gates, *mats
            )
            mixed, grad_rows = mixed + mixed_s, grad_rows + rows_s
            grad_table = grad_table + jnp.where(column[None, :], gates_s[:, None], 0.0)
            kept[s].append(keep)
        mixed_parts.append(mixed.astype(LOW))
        grad_row_parts.append(grad_rows.astype(LOW))
        grad_gate_parts.append(grad_table)
    grad_gates = whole_ring.scatter(grad_gate_parts)
    grad_rows_sum = whole_ring.scatter(grad_row_parts)
    mixture = whole_ring.scatter(mixed_parts)
    layer_out = (residual + mixture).astype(jnp.bfloat16)

    all_rows, all_cot = jnp.concatenate(row_blocks), jnp.concatenate(cot_blocks)
    slab_grads = []
    for keep in kept:
        weighted, grad_gate_pre, grad_up_pre = (
            jnp.concatenate([block[part] for block in keep]) for part in range(3)
        )
        slab_grads.append(
            [
                inner_rows(all_rows, grad_gate_pre).astype(LOW),
                inner_rows(all_rows, grad_up_pre).astype(LOW),
                inner_rows(weighted, all_cot).astype(LOW),
            ]
        )
    expert_grads = [0.0, 0.0, 0.0]
    for shift in range(group_count // 2):
        for part in range(3):
            chip_sum = slab_grads[2 * shift][part].astype(FULL) + swap(
                slab_grads[2 * shift + 1][part], "expert", core_pairs
            ).astype(FULL)
            if shift:
                chip_sum = swap(chip_sum.astype(LOW), "expert", chip_pairs(-shift)).astype(FULL)
            expert_grads[part] = expert_grads[part] + chip_sum

    grad_logits = gate_table * (
        grad_gates - jnp.sum(gate_table * grad_gates, axis=-1, keepdims=True)
    )
    grad_normed_two = grad_rows_sum + outer_rows(grad_logits, w_router.astype(jnp.float32), HIGH)
    grad_router = inner_rows(grad_logits, normed_two.astype(jnp.float32), HIGH)
    grad_unit_two = grad_normed_two * mix_gain
    grad_mix_gain = jnp.sum(grad_normed_two * unit_two, axis=0)
    grad_residual = grad_out + inv_two * (
        grad_unit_two - unit_two * jnp.mean(grad_unit_two * unit_two, axis=-1, keepdims=True)
    )
    grad_branch = grad_residual.astype(jnp.bfloat16)
    grad_branch_all = jnp.concatenate(seq_ring.gather(grad_branch))
    grad_w_out = inner_rows(attn_rows, grad_branch_all)
    grad_attn = outer_rows(grad_branch_all, out_full).astype(jnp.bfloat16)
    grad_items = to_items(grad_attn.reshape(shape_heads))
    grad_query_items, grad_key_items, grad_value_items = lax.map(
        lambda items: attend_back(items, mask),
        (query_items, key_items, value_items, grad_items, log_total),
    )
    grad_value_rows = from_items(grad_value_items).reshape(length, local_width).astype(LOW)

    def prepare_heads(projected, gain_vec):
        return qk_prepare(projected, gain_vec, cos_part, sin_part)

    unused_query, pull_query = jax.vjp(prepare_heads, query_proj, query_gain)
    grad_query_proj, grad_query_gain = pull_query(from_items(grad_query_items))
    unused_key, pull_key = jax.vjp(prepare_heads, key_proj, key_gain)
    grad_key_proj, grad_key_gain = pull_key(from_items(grad_key_items))
    grad_query_low = grad_query_proj.reshape(length, local_width).astype(LOW)
    grad_key_low = grad_key_proj.reshape(length, local_width).astype(LOW)
    partial_normed = [
        (
            outer_rows(grad_query_low[rows], query_full)
            + outer_rows(grad_key_low[rows], key_full)
            + outer_rows(grad_value_rows[rows], value_full)
        ).astype(LOW)
        for rows in (slice(k * tok_rows, (k + 1) * tok_rows) for k in range(part_count))
    ]
    grad_normed_one = seq_ring.scatter(partial_normed)
    grad_weights = [
        inner_rows(normed_all, grad) for grad in (grad_query_low, grad_key_low, grad_value_rows)
    ]
    grad_norm_gain = sum(
        jnp.sum(grad * full.astype(FULL), axis=1)
        for grad, full in zip(grad_weights, (query_full, key_full, value_full))
    ) / norm_gain

    def own_part(grad, axis):
        spread = lax.psum_scatter(
            grad.astype(LOW), "expert", scatter_dimension=1 - axis, tiled=True
        )
        blocks = jnp.split(spread, seq_count, axis=axis)
        total = blocks[0].astype(FULL)
        for s in range(1, seq_count):
            total = total + swap(blocks[s], "tensor", seq_pairs(-s)).astype(FULL)
        return total

    owned_query, owned_key, owned_value = (own_part(grad, 1) for grad in grad_weights)
    owned_out = own_part(grad_w_out, 0)
    grad_unit_one = grad_normed_one * norm_gain
    grad_tokens = grad_residual + inv_one * (
        grad_unit_one - unit_one * jnp.mean(grad_unit_one * unit_one, axis=-1, keepdims=True)
    )
    early_router, early_mix = everywhere((grad_router, grad_mix_gain))
    late_norm, late_query, late_key = everywhere((grad_norm_gain, grad_query_gain, grad_key_gain))
    return (
        layer_out,
        grad_tokens.astype(jnp.bfloat16),
        late_norm,
        owned_query,
        owned_key,
        owned_value,
        late_query,
        late_key,
        owned_out,
        early_mix,
        early_router.T,
        expert_grads[0][None],
        expert_grads[1][None],
        expert_grads[2][None],
    )


def solution(mesh):
    in_specs = (
        P(("expert", "tensor"), None),
        P("expert", None),
        P(("expert", "tensor"), None),
        P(),
        P("expert", "tensor"),
        P("expert", "tensor"),
        P("expert", "tensor"),
        P(),
        P(),
        P("tensor", "expert"),
        P(),
        P(),
        P(("expert", "tensor"), None, None),
        P(("expert", "tensor"), None, None),
        P(("expert", "tensor"), None, None),
        P(("expert", "tensor"), None),
    )
    out_specs = (
        P(("expert", "tensor"), None),
        P(("expert", "tensor"), None),
        P(),
        P("expert", "tensor"),
        P("expert", "tensor"),
        P("expert", "tensor"),
        P(),
        P(),
        P("tensor", "expert"),
        P(),
        P(),
        P(("expert", "tensor"), None, None),
        P(("expert", "tensor"), None, None),
        P(("expert", "tensor"), None, None),
    )
    return jax.shard_map(
        per_device, mesh=mesh, in_specs=in_specs, out_specs=out_specs, check_vma=False
    )
```

```python
import functools

import jax
import jax.numpy as jnp
import numpy as np
from jax import lax
from jax.experimental import pallas as pl
from jax.experimental.pallas import tpu as pltpu
from jax.sharding import PartitionSpec as P

WIN = 1024


EPSILON = 1e-05
THETA = 50000.0
MASKED = -1e30
HIGH = lax.Precision.HIGHEST
LOW = jnp.bfloat16
FULL = jnp.float32
ROOM = 58 << 20
ANYWHERE = pl.BlockSpec(memory_space=pl.ANY)
NEAR = pl.BlockSpec(memory_space=pltpu.VMEM)
Shape = jax.ShapeDtypeStruct


def inner_rows(left_side, right_side, precision=None):
    return lax.dot_general(
        left_side,
        right_side,
        (((0,), (0,)), ((), ())),
        precision=precision,
        preferred_element_type=jnp.float32,
    )


def outer_rows(left_side, right_side, precision=None):
    return lax.dot_general(
        left_side,
        right_side,
        (((1,), (1,)), ((), ())),
        precision=precision,
        preferred_element_type=jnp.float32,
    )


def plain_dot(left_side, right_side):
    return jnp.dot(left_side, right_side, preferred_element_type=jnp.float32)


def cost(flops, moved, exps=0):
    return pl.CostEstimate(
        flops=int(flops) // 3, bytes_accessed=int(moved) // 3, transcendentals=int(exps) // 3
    )


def roomy():
    return pltpu.CompilerParams(vmem_limit_bytes=ROOM)


def fixed_block(shape):
    return pl.BlockSpec(shape, lambda *at: (0,) * len(shape))


def nothing(*refs):
    pass


def after(value, *tokens):
    leaves, tree = jax.tree.flatten(value)
    tokens = jax.tree.leaves(tokens)
    out = pl.pallas_call(
        nothing,
        in_specs=[ANYWHERE] * (len(leaves) + len(tokens)),
        out_specs=[ANYWHERE] * len(leaves),
        out_shape=[Shape(leaf.shape, leaf.dtype) for leaf in leaves],
        input_output_aliases={i: i for i in range(len(leaves))},
        cost_estimate=cost(0, 0),
        name="after",
    )(*leaves, *tokens)
    return jax.tree.unflatten(tree, out)


def fresh_body(value, *refs):
    refs[-1][...] = value[...]


def fresh(value, first, rows, *tokens, steps=2):
    tokens = jax.tree.leaves(tokens)
    step = rows // steps
    at = first // step
    return pl.pallas_call(
        fresh_body,
        grid=(steps,),
        in_specs=[pl.BlockSpec((step, value.shape[1]), lambda i: (at + i, 0))]
        + [ANYWHERE] * len(tokens),
        out_specs=pl.BlockSpec((step, value.shape[1]), lambda i: (i, 0)),
        out_shape=Shape((rows, value.shape[1]), value.dtype),
        compiler_params=roomy(),
        cost_estimate=cost(0, 4 * rows * value.shape[1]),
        name="fresh",
    )(value, *tokens)


def experts_body(blocks, experts, pieces, begun, given, ids_at, spots_at, numbers, *refs):
    refs, slabs = list(refs), len(pieces)

    def take(count):
        return [refs.pop(0) for _ in range(count)]

    rows_in, cot_in = take(blocks), take(blocks)
    mats = [[take(count) for count in counts] for counts in pieces]
    start_rows, start_mixed = take(blocks * begun), take(blocks * begun)
    take(given)
    rows_out, mixed_out, kept_w_out, kept_g_out = take(blocks), take(blocks), *take(2)
    copies = take(0 if begun else 2)
    rows, cot, both, down, rows_sum, mixed_sum, begin, end, kept_w, kept_g, *refs = refs[-15:]
    extra, extra_begin, extra_end, sems, out_sems = refs
    size, hidden, width = rows_in[0].shape[0], down.shape[1], rows.shape[1]
    spans = [pl.ds(b * size, size) for b in range(blocks)]
    spots = [pl.ds(pl.multiple_of(numbers[at], size), size) for at in spots_at]
    loads, stores = [], []

    def load(source, target):
        copy = pltpu.make_async_copy(source, target, sems.at[len(loads)])
        copy.start()
        loads.append(copy)
        return copy

    def store(source, target):
        copy = pltpu.make_async_copy(source, target, out_sems.at[len(stores)])
        copy.start()
        stores.append(copy)

    main, rest = pl.ds(0, width), pl.ds(width, extra.shape[1])
    rows_loads = [load(rows_in[b].at[:, main], rows.at[spans[b]]) for b in range(blocks)]
    extra_loads = [load(rows_in[b].at[:, rest], extra.at[spans[b]]) for b in range(blocks)]
    if begun:
        extra_loads += [
            load(start_rows[b].at[:, rest], extra_begin.at[spans[b]]) for b in range(blocks)
        ]

    def load_mat(parts, target):
        height = parts[0].shape[0]
        return [load(part, target.at[pl.ds(p * height, height)]) for p, part in enumerate(parts)]

    def load_pre(s):
        gate, up, _ = mats[s]
        return load_mat(gate, both.at[s, :, pl.ds(0, hidden)]) + load_mat(
            up, both.at[s, :, pl.ds(hidden, hidden)]
        )

    mat_loads = [load_pre(0)]
    cot_loads = [load(cot_in[b], cot.at[spans[b]]) for b in range(blocks)]
    down_loads = [load_mat(mats[0][2], down.at[0])]
    if begun:
        begin_loads = [
            [load(start_rows[b].at[:, main], begin.at[0, spans[b]]) for b in range(blocks)],
            [load(start_mixed[b], begin.at[1, spans[b]]) for b in range(blocks)],
        ]
    for s in range(1, slabs):
        mat_loads.append(load_pre(s))
        down_loads.append(load_mat(mats[s][2], down.at[s]))
    for copy in extra_loads:
        copy.wait()
    gates = extra[:, :experts].astype(FULL) + extra[:, experts : 2 * experts].astype(FULL)
    table = extra_begin[:, :experts].astype(FULL) if begun else jnp.zeros(gates.shape, FULL)
    for copy in rows_loads:
        copy.wait()
    for s in range(slabs):
        last = s == slabs - 1
        for copy in mat_loads[s]:
            copy.wait()
        pre = plain_dot(rows[...], both[s])
        if s == 0:
            for copy in cot_loads:
                copy.wait()
            for held, copy_out in zip((rows, cot), copies):
                for b in range(blocks):
                    store(held.at[spans[b]], copy_out.at[spots[b]])
        for copy in down_loads[s]:
            copy.wait()
        plain_grad = outer_rows(cot[...], down[s])
        hit = lax.broadcasted_iota(jnp.int32, gates.shape, 1) == numbers[ids_at[s]]
        gate = jnp.sum(jnp.where(hit, gates, 0.0), axis=1, keepdims=True)
        gate_pre, up_pre = pre[:, :hidden], pre[:, hidden:]
        sigmoid_val = 0.5 * jnp.tanh(0.5 * gate_pre) + 0.5
        silu_val = gate_pre * sigmoid_val
        activation = (silu_val * up_pre).astype(LOW).astype(FULL)
        table = table + jnp.where(
            hit, jnp.sum(activation * plain_grad, axis=1, keepdims=True), 0.0
        )
        grad_act = gate * plain_grad
        kept_w[s] = (gate * activation).astype(LOW)
        kept_g[s, :, :hidden] = (
            grad_act * up_pre * (sigmoid_val + silu_val * (1.0 - sigmoid_val))
        ).astype(LOW)
        kept_g[s, :, hidden:] = (grad_act * silu_val).astype(LOW)
        for b in range(blocks):
            store(kept_w.at[s, spans[b]], kept_w_out.at[spots[b], pl.ds(s * hidden, hidden)])
            store(
                kept_g.at[s, spans[b]], kept_g_out.at[spots[b], pl.ds(2 * s * hidden, 2 * hidden)]
            )
        for i, sums in enumerate((rows_sum, mixed_sum)):
            if s == 0 and begun:
                for copy in begin_loads[i]:
                    copy.wait()
            for p in range(2):
                columns = pl.ds(p * (width // 2), width // 2)
                if i == 0:
                    part = outer_rows(kept_g[s], both[s, columns, :])
                else:
                    part = plain_dot(kept_w[s], down[s, :, columns])
                if s > 0:
                    part = part + sums[:, columns]
                elif begun:
                    part = part + begin[i, :, columns].astype(FULL)
                if last:
                    end[i, :, columns] = part.astype(LOW)
                    for b in range(blocks):
                        out = (rows_out, mixed_out)[i][b]
                        store(end.at[i, spans[b], columns], out.at[:, columns])
                else:
                    sums[:, columns] = part
    extra_end[...] = jnp.zeros(extra_end.shape, LOW)
    extra_end[:, :experts] = table.astype(LOW)
    for b in range(blocks):
        store(extra_end.at[spans[b]], rows_out[b].at[:, rest])
    for copy in stores:
        copy.wait()


def experts_call(
    experts, numbers, ids_at, spots_at, rows, cot, mats, start, shared, total_rows, tokens
):
    blocks, slabs = len(rows), len(mats)
    size, width = cot[0].shape
    extra = rows[0].shape[1] - width
    hidden, total = mats[0][0][0].shape[1], blocks * size
    pieces = [[len(parts) for parts in trio] for trio in mats]
    piece_count = sum(map(sum, pieces))
    operands = [numbers, *rows, *cot]
    specs = [pl.BlockSpec(memory_space=pltpu.SMEM)] + [ANYWHERE] * (2 * blocks)
    for trio in mats:
        operands += [part for parts in trio for part in parts]
    specs += [ANYWHERE] * piece_count
    if start is not None:
        operands += [*start[0], *start[1]]
        specs += [ANYWHERE] * (2 * blocks)
    aliases, given = {}, 0
    outs = 2 * blocks
    for j, part in enumerate(shared):
        if part is not None:
            aliases[len(operands)] = outs + j
            operands.append(part)
            specs.append(ANYWHERE)
            given += 1
    given += len(tokens)
    operands += tokens
    specs += [ANYWHERE] * len(tokens)
    wide, hidden_all = Shape((total_rows, width), LOW), slabs * hidden
    out = pl.pallas_call(
        functools.partial(
            experts_body,
            blocks,
            experts,
            pieces,
            int(start is not None),
            given,
            ids_at,
            spots_at,
        ),
        in_specs=specs,
        out_specs=[ANYWHERE] * (outs + len(shared)),
        out_shape=[Shape((size, width + extra), LOW)] * blocks
        + [Shape((size, width), LOW)] * blocks
        + [Shape((total_rows, hidden_all), LOW), Shape((total_rows, 2 * hidden_all), LOW)]
        + [wide] * (len(shared) - 2),
        input_output_aliases=aliases,
        scratch_shapes=[
            pltpu.VMEM((total, width), LOW),
            pltpu.VMEM((total, width), LOW),
            pltpu.VMEM((slabs, width, 2 * hidden), LOW),
            pltpu.VMEM((slabs, hidden, width), LOW),
            pltpu.VMEM((total, width), FULL),
            pltpu.VMEM((total, width), FULL),
            pltpu.VMEM((2, total, width), LOW),
            pltpu.VMEM((2, total, width), LOW),
            pltpu.VMEM((slabs, total, hidden), LOW),
            pltpu.VMEM((slabs, total, 2 * hidden), LOW),
            pltpu.VMEM((total, extra), LOW),
            pltpu.VMEM((total, extra), LOW),
            pltpu.VMEM((total, extra), LOW),
            pltpu.SemaphoreType.DMA((6 * blocks + piece_count,)),
            pltpu.SemaphoreType.DMA((2 * slabs * blocks + 7 * blocks,)),
        ],
        compiler_params=roomy(),
        cost_estimate=cost(
            12 * total * width * hidden * slabs,
            6 * width * hidden * slabs + 8 * total * width + 6 * total * hidden * slabs,
            total * hidden * slabs,
        ),
        name="experts",
    )(*operands)
    return out[:blocks], out[blocks:outs], out[outs:]


def slab_grads_body(swapped, parts, term_count, rows, kept, *refs):
    terms, outs = refs[: term_count * parts], refs[-parts:]
    found = inner_rows(kept[...], rows[...])
    if swapped:
        found = found.astype(LOW).T.astype(FULL)
    steps = pl.num_programs(0) // parts

    def put(part):
        total = found
        for term in terms[part::parts]:
            total = total + term[...].astype(FULL)
        outs[part][...] = total.astype(LOW)

    for part in range(parts):
        pl.when(pl.program_id(0) // steps == part)(functools.partial(put, part))


def slab_grads_call(rows, kept, first, count, parts, swapped, terms, tokens, step=256):
    total, width = rows.shape
    at, steps = first // step, count // step

    def spec(part):
        def place(i):
            return jnp.clip(i - part * steps, 0, steps - 1)

        if swapped:
            return pl.BlockSpec((width, step), lambda i: (0, place(i)))
        return pl.BlockSpec((step, width), lambda i: (place(i), 0))

    specs = [spec(part) for part in range(parts)]
    return pl.pallas_call(
        functools.partial(slab_grads_body, swapped, parts, len(terms)),
        grid=(parts * steps,),
        in_specs=[
            pl.BlockSpec((total, width), lambda i: (0, 0), pipeline_mode=pl.Buffered(1)),
            pl.BlockSpec((total, step), lambda i: (0, at + i)),
        ]
        + specs * len(terms)
        + [ANYWHERE] * len(tokens),
        out_specs=specs,
        out_shape=[Shape((width, count) if swapped else (count, width), LOW)] * parts,
        compiler_params=roomy(),
        cost_estimate=cost(
            2 * total * width * count * parts,
            2 * total * width + 2 * (total + width) * count * parts,
        ),
        name="slab_grads",
    )(rows, kept, *[part for term in terms for part in term], *tokens)


def rope_tables(length, head_size):
    half_size = head_size // 2
    frequency = THETA ** (-2.0 * np.arange(half_size) / head_size)
    angles = np.arange(length)[:, None] * frequency[None, :]
    cos_part, sin_part = np.cos(angles), np.sin(angles)
    return np.concatenate([cos_part, cos_part, -sin_part, sin_part], axis=1).astype(np.float32)


def half_turn(vectors):
    return pltpu.roll(vectors, vectors.shape[1] // 2, 1)


def project_body(rows, query, query_rest, key, key_rest, value, value_rest, gains, tables, *refs):
    query_proj, query_low, key_proj, key_low, value_low = refs
    half = query.shape[0]

    def both_halves(mat, rest):
        return plain_dot(rows[:, :half], mat[...]) + plain_dot(rows[:, half:], rest[...])

    size = gains.shape[1]
    cos_two, sin_two = tables[:, :size], tables[:, size:]
    for mat, rest, gain, proj_out, low_out in (
        (query, query_rest, gains[0:1], query_proj, query_low),
        (key, key_rest, gains[1:2], key_proj, key_low),
    ):
        proj = both_halves(mat, rest)
        proj_out[...] = proj
        for h in range(mat.shape[1] // size):
            columns = slice(h * size, (h + 1) * size)
            head = proj[:, columns]
            head = head * lax.rsqrt(jnp.mean(head * head, axis=-1, keepdims=True) + EPSILON)
            head = head * gain
            low_out[:, columns] = (head * cos_two + half_turn(head) * sin_two).astype(LOW)
    value_low[...] = both_halves(value, value_rest).astype(LOW)


def project_call(rows, mats, gains, tables):
    total, width = rows.shape
    mats = [half for halves in mats for half in halves]
    columns, step = mats[0].shape[1], min(256, total)
    row_block = pl.BlockSpec((step, columns), lambda i: (i, 0))
    full, low = Shape((total, columns), FULL), Shape((total, columns), LOW)
    return pl.pallas_call(
        project_body,
        grid=(total // step,),
        in_specs=[pl.BlockSpec((step, width), lambda i: (i, 0))]
        + [fixed_block(mat.shape) for mat in mats]
        + [fixed_block(gains.shape), pl.BlockSpec((step, tables.shape[1]), lambda i: (i, 0))],
        out_specs=[row_block] * 5,
        out_shape=[full, low, full, low, low],
        compiler_params=roomy(),
        cost_estimate=cost(
            6 * total * width * columns, 2 * total * width + 6 * width * columns + 14 * total * columns
        ),
        name="project",
    )(rows, *mats, gains, tables)


def held_pairs(seg_col, seg_row, pos_col, pos_row):
    same = seg_col == seg_row
    if seg_row.shape[1] > WIN:
        same = same & (jnp.abs(pos_col - pos_row) < WIN)
    return same


def softmax_rows(query, key, held):
    scores = outer_rows(query, key) * (query.shape[1] ** -0.5)
    scores = jnp.where(held, scores, MASKED)
    raised = jnp.exp(scores - jnp.max(scores, axis=-1, keepdims=True))
    return raised * (1.0 / jnp.sum(raised, axis=-1, keepdims=True))


def attend_body(query, key, value, seg_col, seg_row, pos_col, pos_row, *refs):
    out = refs[-1]
    held = held_pairs(seg_col[...], seg_row[...], pos_col[...], pos_row[...])
    probs = softmax_rows(query[...], key[...], held).astype(LOW)
    out[...] = plain_dot(probs, value[...]).astype(LOW)


def attend_call(query, key, value, places, size, first, rows, tokens):
    total, columns = query.shape
    heads = columns // size
    at = first // rows
    column_block = pl.BlockSpec((total, size), lambda h: (0, h))
    col = pl.BlockSpec((rows, 1), lambda h: (at, 0))
    row = fixed_block((1, total))
    return pl.pallas_call(
        attend_body,
        grid=(heads,),
        in_specs=[
            pl.BlockSpec((rows, size), lambda h: (at, h)),
            column_block,
            column_block,
            col,
            row,
            col,
            row,
        ]
        + [ANYWHERE] * len(tokens),
        out_specs=pl.BlockSpec((rows, size), lambda h: (0, h)),
        out_shape=Shape((rows, columns), LOW),
        compiler_params=roomy(),
        cost_estimate=cost(
            4 * rows * total * columns, 4 * (total + rows) * columns, rows * total * heads
        ),
        name="attend",
    )(query, key, value, *places, *tokens)


def unprepare(grad, proj, gain, cos_two, sin_two):
    inverse = lax.rsqrt(jnp.mean(proj * proj, axis=-1, keepdims=True) + EPSILON)
    unit = proj * inverse
    grad = grad * cos_two + half_turn(grad * sin_two)
    gain_grad = jnp.sum(grad * unit, axis=0, keepdims=True)
    grad = grad * gain
    return inverse * (grad - unit * jnp.mean(grad * unit, axis=-1, keepdims=True)), gain_grad


def attend_back_body(
    step,
    query,
    key,
    value,
    grad,
    query_proj,
    key_proj,
    gains,
    tables,
    seg_col,
    seg_row,
    pos_col,
    pos_row,
    grad_query,
    grad_key,
    grad_value,
    grad_gains,
    query_sum,
    key_sum,
    value_sum,
):
    total, size = query.shape
    scaling = size**-0.5
    for q in range(total // step):
        at = pl.ds(q * step, step)
        held = held_pairs(seg_col[at], seg_row[...], pos_col[at], pos_row[...])
        probs = softmax_rows(query[at], key[...], held)
        grad_probs = outer_rows(grad[at], value[...]).astype(LOW).astype(FULL)
        weighted = probs * grad_probs
        centre = jnp.sum(weighted, axis=-1, keepdims=True)
        grad_scores = (weighted - probs * centre).astype(LOW)
        query_sum[at] = plain_dot(grad_scores, key[...]) * scaling
        key_part = inner_rows(grad_scores, query[at])
        value_part = inner_rows(probs.astype(LOW), grad[at])
        if q == 0:
            key_sum[...] = key_part
            value_sum[...] = value_part
        else:
            key_sum[...] += key_part
            value_sum[...] += value_part
    grad_value[...] = value_sum[...].astype(LOW)
    turns = (tables[:, :size], tables[:, size:])
    query_part, query_gain_part = unprepare(
        query_sum[...], query_proj[...], gains[0:1], *turns
    )
    key_part, key_gain_part = unprepare(
        key_sum[...] * scaling, key_proj[...], gains[1:2], *turns
    )
    grad_query[...] = query_part.astype(LOW)
    grad_key[...] = key_part.astype(LOW)

    @pl.when(pl.program_id(0) == 0)
    def _():
        grad_gains[...] = jnp.zeros_like(grad_gains)

    grad_gains[0:1] += query_gain_part
    grad_gains[1:2] += key_gain_part


def attend_back_call(query, key, value, grad, query_proj, key_proj, gains, tables, places):
    total, columns = query.shape
    size = gains.shape[1]
    heads, step = columns // size, min(256, total)
    head = pl.BlockSpec((total, size), lambda h: (0, h))
    fixed = (gains, tables, *places)
    return pl.pallas_call(
        functools.partial(attend_back_body, step),
        grid=(heads,),
        in_specs=[head] * 6 + [fixed_block(a.shape) for a in fixed],
        out_specs=[head] * 3 + [fixed_block((2, size))],
        out_shape=[Shape((total, columns), LOW)] * 3 + [Shape((2, size), FULL)],
        scratch_shapes=[pltpu.VMEM((total, size), FULL)] * 3,
        compiler_params=roomy(),
        cost_estimate=cost(
            10 * total * total * columns, 22 * total * columns, total * total * heads
        ),
        name="attend_back",
    )(query, key, value, grad, query_proj, key_proj, *fixed)


def rows_back_body(count, *refs):
    grads, firsts, rests = (refs[k * count : (k + 1) * count] for k in range(3))
    outs = refs[3 * count :]
    step, steps, size = pl.program_id(0), pl.num_programs(0), outs[0].shape[0]

    def run(mats):
        total = outer_rows(grads[0][...], mats[0][...])
        for grad, mat in zip(grads[1:], mats[1:]):
            total = total + outer_rows(grad[...], mat[...])
        for b, out in enumerate(outs):
            out[...] = total[b * size : (b + 1) * size].astype(LOW)

    pl.when(step < steps // 2)(lambda: run(firsts))
    pl.when(step >= steps // 2)(lambda: run(rests))


def rows_back_call(grads, mats, size, tokens):
    (rows, columns), count = grads[0].shape, len(grads)
    half, blocks = mats[0][0].shape[0], rows // size
    step = half // 2

    def body(*refs):
        rows_back_body(count, *refs[: 3 * count], *refs[3 * count + len(tokens) :])

    return pl.pallas_call(
        body,
        grid=(4,),
        in_specs=[fixed_block((rows, columns))] * count
        + [pl.BlockSpec((step, columns), lambda i: (jnp.minimum(i, 1), 0))] * count
        + [pl.BlockSpec((step, columns), lambda i: (jnp.maximum(i - 2, 0), 0))] * count
        + [ANYWHERE] * len(tokens),
        out_specs=[pl.BlockSpec((size, step), lambda i: (0, i))] * blocks,
        out_shape=[Shape((size, 2 * half), LOW)] * blocks,
        compiler_params=roomy(),
        cost_estimate=cost(
            4 * count * rows * columns * half,
            2 * count * (rows * columns + 2 * columns * half) + 4 * rows * half,
        ),
        name="rows_back",
    )(*grads, *[mat[0] for mat in mats], *[mat[1] for mat in mats], *tokens)


def weight_back_body(columns, rows, branch, query, key, value, attended, *refs):
    out = refs[-1]
    for place, (left, right) in enumerate(
        ((rows, query), (rows, key), (rows, value), (branch, attended))
    ):
        out[:, place * columns : (place + 1) * columns] = inner_rows(
            left[...], right[...]
        ).astype(LOW)


def weight_back_call(rows, branch, grads, attended, half, tokens, step=512):
    (total, width), columns = rows.shape, attended.shape[1]
    steps = width // 2 // step
    part = pl.BlockSpec((total, step), lambda i: (0, half * steps + i))
    return pl.pallas_call(
        functools.partial(weight_back_body, columns),
        grid=(steps,),
        in_specs=[part, part] + [fixed_block((total, columns))] * 4 + [ANYWHERE] * len(tokens),
        out_specs=pl.BlockSpec((step, 4 * columns), lambda i: (i, 0)),
        out_shape=Shape((width // 2, 4 * columns), LOW),
        compiler_params=roomy(),
        cost_estimate=cost(
            4 * total * width * columns, 2 * total * width + 8 * (total + width // 2) * columns
        ),
        name="weight_back",
    )(rows, branch, *grads, attended, *tokens)


class Ring:
    def __init__(self, axis, size, count):
        self.axis, self.count = axis, count
        self.order = list(range(0, count, 2)) + list(range(count - 1, 0, -2))
        self.rightward = [
            (base + self.order[k], base + self.order[(k + 1) % count])
            for base in range(0, size, count)
            for k in range(count)
        ]
        self.leftward = [(to, start) for start, to in self.rightward]

    def right(self, value):
        return jax.tree.map(lambda v: lax.ppermute(v, self.axis, self.rightward), value)

    def left(self, value):
        return jax.tree.map(lambda v: lax.ppermute(v, self.axis, self.leftward), value)

    def members(self, at):
        count = self.count
        spot = jnp.where(at % 2 == 0, at // 2, count - (at + 1) // 2)
        shifts = [0]
        for k in range(1, count // 2):
            shifts += [-k, k]
        shifts.append(count // 2)
        spots = [(spot + shift + count) % count for shift in shifts]
        return [jnp.where(p < count // 2, 2 * p, 2 * (count - p) - 1) for p in spots]

    def gather(self, value, use, between):
        from_left = from_right = value
        use(0, [value])
        for k in range(1, self.count // 2):
            from_left, from_right = between(k, (self.right(from_left), self.left(from_right)))
            use(k, [from_left, from_right])
        upper = self.right(jax.tree.map(lambda v: v[: v.shape[0] // 2], from_left))
        lower = self.left(jax.tree.map(lambda v: v[v.shape[0] // 2 :], from_right))
        upper, lower = between(self.count // 2, (upper, lower))
        use(
            self.count // 2,
            [jax.tree.map(lambda u, v: jnp.concatenate([u, v]), upper, lower)],
        )

    def scatter(self, make, finish=lambda pair: pair):
        steps = Reduction(self)
        tokens = []
        for k in range(self.count // 2, 0, -1):
            tokens = steps.hop(make(k, tokens))
        (own,) = make(0, tokens)
        steps.pair = finish(steps.pair)
        return steps.total(own)


class Spread:
    def __init__(self, ring, value):
        self.ring, self.pair, self.blocks, self.hops = ring, (value, value), [value], 0

    def hop(self, *tokens):
        ring = self.ring
        if self.hops:
            self.settle(*tokens)
        left, right = self.pair
        self.hops += 1
        if self.hops == ring.count // 2:
            left, right = left[: left.shape[0] // 2], right[right.shape[0] // 2 :]
        self.pair = (ring.right(left), ring.left(right))

    def settle(self, *tokens):
        self.pair = after(self.pair, *tokens)
        if self.hops == self.ring.count // 2:
            self.blocks.append(jnp.concatenate(self.pair))
        else:
            self.blocks.extend(self.pair)


class Reduction:
    def __init__(self, ring):
        self.ring, self.pair = ring, None

    def hop(self, terms, *tokens):
        ring = self.ring
        if self.pair is None:
            (far,) = terms
            if tokens:
                far = after(far, *tokens)
            half = far.shape[0] // 2
            sent = [far]
            self.pair = (ring.right(far[:half]), ring.left(far[half:]))
        else:
            on_left, on_right = terms
            from_left, from_right = self.pair
            half = from_left.shape[0]
            if half < on_left.shape[0]:
                to_right = jnp.concatenate([on_right[:half] + from_left, on_right[half:]])
                to_left = jnp.concatenate([on_left[:half], on_left[half:] + from_right])
            else:
                to_right, to_left = on_right + from_left, on_left + from_right
            sent = [to_right, to_left]
            if tokens:
                sent = after(sent, *tokens)
            self.pair = (ring.right(sent[0]), ring.left(sent[1]))
        return sent

    def total(self, own):
        return own.astype(FULL) + self.pair[0].astype(FULL) + self.pair[1].astype(FULL)


class Owners:
    def __init__(self):
        self.count = lax.axis_size("expert")
        self.chips = self.count // 2
        self.here = lax.axis_index("expert")

    def cross(self, value):
        pairs = [(i, i ^ 1) for i in range(self.count)]
        return jax.tree.map(lambda v: lax.ppermute(v, "expert", pairs), value)

    def along(self, value, shift):
        pairs = [(i, (i + 2 * shift) % self.count) for i in range(self.count)]
        return jax.tree.map(lambda v: lax.ppermute(v, "expert", pairs), value)

    def listed(self):
        chip, core = self.here // 2, self.here % 2
        return [
            (chip - shift + self.chips) % self.chips * 2 + (core ^ other)
            for other in range(2)
            for shift in range(self.chips)
        ]

    def places(self):
        chip, core = self.here // 2, self.here % 2
        return [
            (core ^ (at % 2)) * self.chips + (chip - at // 2 + self.chips) % self.chips
            for at in range(self.count)
        ]

    def scatter(self, parts):
        mine, other = parts[: self.chips], parts[self.chips :]
        other = self.cross(jnp.concatenate(other, axis=0))
        rows = mine[0].shape[0]
        total = None
        for shift in reversed(range(self.chips)):
            part = mine[shift].astype(FULL) + other[shift * rows : (shift + 1) * rows].astype(FULL)
            if shift:
                part = self.along(part.astype(LOW), -shift).astype(FULL)
            total = part if total is None else total + part
        return total

    def pick_columns(self, rows, places):
        size = rows.shape[1] // self.count
        return jnp.concatenate(
            [lax.dynamic_slice_in_dim(rows, at * size, size, 1) for at in places], axis=1
        )

    def list_columns(self, rows):
        return self.pick_columns(rows, self.listed())

    def unlist_columns(self, rows):
        return self.pick_columns(rows, self.places())


def everywhere(value):
    for axis in ("expert", "tensor"):
        size, step = lax.axis_size(axis), 1
        while step < size:
            pairs = [(i, i ^ step) for i in range(size)]
            value = jax.tree.map(lambda v: v + lax.ppermute(v, axis, pairs), value)
            step *= 2
    return value


def per_device(
    tokens,
    segments,
    routes,
    norm_gain,
    w_query,
    w_key,
    w_value,
    query_gain,
    key_gain,
    w_out,
    mix_gain,
    w_router,
    w_gate,
    w_up,
    w_down,
    cotangent,
):
    tensor_count = lax.axis_size("tensor")
    expert_count = w_router.shape[1]
    tok_rows, model_width = tokens.shape
    seq_count, length = segments.shape
    head_size = query_gain.shape[0]
    part_count = tensor_count // seq_count
    block_width = w_query.shape[1]
    local_width = seq_count * block_width
    tensor_at = lax.axis_index("tensor")
    seq_at, part_at = tensor_at // part_count, tensor_at % part_count
    whole_ring = Ring("tensor", tensor_count, tensor_count)
    seq_ring = Ring("tensor", tensor_count, part_count)
    owners = Owners()

    def seq_swap(value, shift):
        pairs = [(t, (t + part_count * shift) % tensor_count) for t in range(tensor_count)]
        return lax.ppermute(value, "tensor", pairs)

    inputs = tokens.astype(jnp.float32)
    inv_one = lax.rsqrt(jnp.mean(inputs * inputs, axis=-1, keepdims=True) + EPSILON)
    unit_one = inputs * inv_one
    normed_one = owners.list_columns((unit_one * norm_gain).astype(jnp.bfloat16))

    seq_shifts, chip_shifts = range(1, seq_count), range(1, owners.chips)
    hidden, total_rows = w_down.shape[1], tensor_count * tok_rows
    own_slab = (w_gate[0], w_up[0], w_down[0])
    copies = [
        fresh(cotangent, 0, tok_rows, normed_one),
        fresh(own_slab[0], 0, model_width, normed_one),
        fresh(own_slab[1], 0, model_width, normed_one),
        fresh(own_slab[2], 0, hidden // 2, normed_one),
        fresh(own_slab[2], hidden // 2, hidden // 2, normed_one),
    ]
    query_key = jnp.concatenate([w_query, w_key], axis=1)
    wave = [
        *[seq_swap(query_key, s) for s in seq_shifts],
        *[owners.along(w, s) for w in (w_value, w_out) for s in chip_shifts],
    ]
    gathered, found = [], {}

    def between(k, pair):
        nonlocal wave
        if k == 1:
            pair, moved, copies[:] = after((pair, wave, copies))
            moved, others = moved[seq_count - 1 :], moved[: seq_count - 1]
            heads = [query_key, *others]
            found["pair"] = jnp.concatenate(
                [h[:, :block_width] for h in heads] + [h[:, block_width:] for h in heads], axis=1
            )
            count = owners.chips - 1
            found["value"] = jnp.concatenate([w_value, *moved[:count]], axis=0)
            found["out"] = jnp.concatenate([w_out, *moved[count:]], axis=1)
            wave = [
                *[owners.along(found["pair"], s) for s in chip_shifts],
                *[seq_swap(found["value"], s) for s in seq_shifts],
            ]
        elif k == part_count // 2:
            pair, moved = after((pair, wave))
            count = owners.chips - 1
            found["pair"] = jnp.concatenate([found["pair"], *moved[:count]], axis=0)
            found["value"] = jnp.concatenate([found["value"], *moved[count:]], axis=1)
            wave = moved[:1]
        return pair

    seq_ring.gather(normed_one, lambda k, blocks: gathered.extend(blocks), between)
    normed_all = jnp.concatenate(gathered)
    pair_rest, value_rest = owners.cross(found["pair"]), owners.cross(found["value"])
    full_mats = [
        (found["pair"][:, :local_width], pair_rest[:, :local_width]),
        (found["pair"][:, local_width:], pair_rest[:, local_width:]),
        (found["value"], value_rest),
    ]
    own_cot, own_gate, own_up, *own_down = copies
    cot_steps = Spread(whole_ring, after(own_cot, wave))
    cot_steps.hop()
    far_gate = [owners.along(after(own_gate, wave), s) for s in chip_shifts]
    far_up = [owners.along(after(own_up, far_gate), s) for s in chip_shifts]

    whole_members = whole_ring.members(tensor_at)
    seq_members = seq_ring.members(part_at)
    numbers = jnp.stack(
        [at * tok_rows for at in whole_members]
        + [(at * tensor_count + tensor_at) // 2 for at in owners.listed()]
    )
    ids_from = tensor_count

    def from_place(table):
        return jnp.concatenate(
            [
                lax.dynamic_slice_in_dim(table, at * tok_rows, tok_rows, 0)
                for at in seq_members
            ]
        )

    tables = from_place(jnp.array(rope_tables(length, head_size)))
    seg_row = lax.dynamic_index_in_dim(segments, seq_at, 0, keepdims=False)
    marks = from_place(jnp.stack([seg_row, jnp.arange(length, dtype=jnp.int32)], axis=1))
    places = (marks[:, :1], marks[:, :1].T, marks[:, 1:], marks[:, 1:].T)
    gains = jnp.stack([query_gain, key_gain])

    query_proj, query_low, key_proj, key_low, value_low = project_call(
        normed_all, full_mats, gains, tables
    )

    def place_of(ring, k):
        return {0: [0], ring.count // 2: [ring.count - 1]}.get(k, [2 * k - 1, 2 * k])

    cot_steps.hop(query_low)
    out_chips = after(found["out"], pair_rest)
    out_heads = jnp.concatenate(
        [out_chips, *after([seq_swap(out_chips, s) for s in seq_shifts], query_low)], axis=0
    )
    out_full = jnp.concatenate([out_heads, owners.cross(out_heads)], axis=1)
    attended = [None] * part_count

    def branch_parts(k, tokens):
        parts = []
        tokens = list(tokens) + (far_gate if k == 0 else [])
        for b in place_of(seq_ring, k):
            attended[b] = attend_call(
                query_low,
                key_low,
                value_low,
                places,
                head_size,
                b * tok_rows,
                tok_rows,
                tokens,
            )
            parts.append(plain_dot(attended[b], out_full).astype(LOW))
        return parts

    def branch_done(pair):
        cot_steps.hop(pair)
        return pair

    residual = inputs + owners.unlist_columns(seq_ring.scatter(branch_parts, branch_done))
    attn_rows = jnp.concatenate(attended)
    inv_two = lax.rsqrt(jnp.mean(residual * residual, axis=-1, keepdims=True) + EPSILON)
    unit_two = residual * inv_two
    normed_two = (unit_two * mix_gain).astype(jnp.bfloat16)
    logits = jnp.dot(normed_two, w_router, preferred_element_type=jnp.float32)
    hits = jnp.any(
        routes[:, :, None] == jnp.arange(expert_count, dtype=jnp.int32)[None, None, :], axis=1
    )
    top_logit = jnp.max(jnp.where(hits, logits, MASKED), axis=-1, keepdims=True)
    raised = jnp.where(hits, jnp.exp(logits - top_logit), 0.0)
    gate_table = raised / jnp.sum(raised, axis=-1, keepdims=True)

    grad_out = cotangent.astype(jnp.float32)
    far_down = []
    slab_mats = {0: [[[w] for w in own_slab], [[w] for w in owners.cross(own_slab)]]}
    row_blocks, sums, mixed = ([None] * tensor_count for _ in range(3))
    shared_all = []

    def run_experts(shift, k, tokens):
        at = place_of(whole_ring, k)
        if len(shared_all) == shift:
            shared_all.append([None] * (2 if shift else 4))
        parts, mixed_parts, shared_all[shift] = experts_call(
            expert_count,
            numbers,
            [ids_from + shift, ids_from + owners.chips + shift],
            at,
            [row_blocks[b] for b in at],
            [cot_steps.blocks[b] for b in at],
            slab_mats[shift],
            [[part[b] for b in at] for part in (sums, mixed)] if shift else None,
            shared_all[shift],
            total_rows,
            tokens,
        )
        for b, part, mixed_part in zip(at, parts, mixed_parts):
            sums[b], mixed[b] = part, mixed_part
        return [sums[b] for b in at]

    def first_pair(k, blocks):
        for b, rows in zip(place_of(whole_ring, k), blocks):
            row_blocks[b] = rows
        run_experts(0, k, [])

    def next_hop(k, pair):
        done = [sums[b] for b in place_of(whole_ring, k - 1)]
        if k == 1:
            while cot_steps.hops < tensor_count // 2:
                cot_steps.hop(pair)
            pair, far_up[:] = after((pair, far_up), *done)
        elif k <= 3:
            pair, far_down[-1] = after((pair, far_down[-1]), *done)
            if k == 2:
                cot_steps.settle(pair)
        elif k < tensor_count // 2:
            pair = after(pair, *done)
        if k <= 2:
            piece = after(own_down[k - 1], pair[0])
            far_down.append([owners.along(piece, s) for s in chip_shifts])
        return pair

    high = lax.reduce_precision(gate_table, 8, 7)
    room = -2 * expert_count % 128
    payload = jnp.concatenate(
        [
            normed_two,
            high.astype(LOW),
            (gate_table - high).astype(LOW),
            jnp.zeros((tok_rows, room), LOW),
        ],
        axis=1,
    )
    whole_ring.gather(payload, first_pair, next_hop)
    for shift in chip_shifts:
        mine = [[far_gate[shift - 1]], [far_up[shift - 1]], [piece[shift - 1] for piece in far_down]]
        slab_mats[shift] = [mine, owners.cross(mine)]
    for shift in range(1, owners.chips - 1):
        for k in range(tensor_count // 2 + 1):
            run_experts(shift, k, [])

    def last_pair(k, tokens):
        return run_experts(owners.chips - 1, k, jax.tree.leaves(tokens))

    def down_grads(shift, other, terms, tokens):
        kept, all_cot = shared_all[shift][0], shared_all[0][3]
        return slab_grads_call(
            all_cot, kept, other * hidden, hidden, 1, False, [[t] for t in terms], tokens
        )[0]

    def pre_grads(shift, other, terms, tokens):
        kept, rows = shared_all[shift][1], shared_all[0][2]
        return slab_grads_call(
            rows, kept, 2 * other * hidden, hidden, 2, True, terms, tokens
        )

    def far_down_grads(tokens):
        others = [owners.cross(down_grads(s, 1, [], tokens)) for s in chip_shifts]
        return [down_grads(s, 0, [other], tokens) for s, other in zip(chip_shifts, others)]

    def finish(pair):
        pair, found["down"] = after((pair, far_down_grads([sums[0]])))
        return pair

    summed_rows = whole_ring.scatter(last_pair, finish)
    grad_rows_sum = summed_rows[:, :model_width]
    grad_gates = summed_rows[:, model_width : model_width + expert_count]
    sent_down = [owners.along(part, -s) for s, part in zip(chip_shifts, found["down"])]

    grad_logits = gate_table * (
        grad_gates - jnp.sum(gate_table * grad_gates, axis=-1, keepdims=True)
    )
    grad_normed_two = grad_rows_sum + outer_rows(grad_logits, w_router.astype(jnp.float32), HIGH)
    grad_router = inner_rows(grad_logits, normed_two.astype(jnp.float32), HIGH)
    grad_unit_two = grad_normed_two * mix_gain
    grad_mix_gain = jnp.sum(grad_normed_two * unit_two, axis=0)
    grad_residual = grad_out + inv_two * (
        grad_unit_two - unit_two * jnp.mean(grad_unit_two * unit_two, axis=-1, keepdims=True)
    )
    grad_branch = owners.list_columns(grad_residual.astype(jnp.bfloat16))
    gathered_back = []

    def back_hop(k, pair):
        if k == 1:
            others = [owners.cross(pre_grads(s, 1, [], [grad_branch])) for s in chip_shifts]
            pair = after(pair)
            found["pre"] = [
                pre_grads(s, 0, [other], [pair[0]]) for s, other in zip(chip_shifts, others)
            ]
        elif k == part_count // 2:
            pair, sent_down[:] = after((pair, sent_down), found["pre"])
        return pair

    seq_ring.gather(grad_branch, lambda k, blocks: gathered_back.extend(blocks), back_hop)
    sent_gate = [owners.along(part[0], -s) for s, part in zip(chip_shifts, found["pre"])]
    mixture_steps = Reduction(whole_ring)
    mixture_steps.hop(mixed[-1:], gathered_back[-1])
    grad_attn = jnp.concatenate(
        [outer_rows(block, out_full).astype(jnp.bfloat16) for block in gathered_back]
    )
    *head_grads, grad_gains = attend_back_call(
        query_low, key_low, value_low, grad_attn, query_proj, key_proj, gains, tables, places
    )

    def mixture_hop(k, *tokens):
        mixture_steps.hop([mixed[b] for b in place_of(whole_ring, k)], *tokens)

    mixture_hop(tensor_count // 2 - 1, head_grads[0])
    grad_branch_all = jnp.concatenate(gathered_back)
    own_other_half = weight_back_call(
        normed_all, grad_branch_all, head_grads, attn_rows, 1, []
    )
    other_half = owners.cross(own_other_half)
    mine_half = weight_back_call(
        normed_all, grad_branch_all, head_grads, attn_rows, 0, [own_other_half]
    )
    normed_parts = rows_back_call(head_grads, full_mats, tok_rows, [mine_half, *sent_gate])
    own_other_down = owners.cross(down_grads(0, 1, [], [normed_parts[0]]))
    chip_rows = model_width // owners.count
    piece_rows = chip_rows // 2
    pieces = [slice(p * piece_rows, (p + 1) * piece_rows) for p in range(2)]

    def both_cores(shift, rows, columns=slice(None)):
        rows = slice(shift * chip_rows + rows.start, shift * chip_rows + rows.stop)
        return mine_half[rows, columns].astype(FULL) + other_half[rows, columns].astype(FULL)

    sent_parts = [[both_cores(s, rows).astype(LOW) for s in chip_shifts] for rows in pieces]
    come = []

    def give_parts(k, tokens):
        parts = [normed_parts[b] for b in place_of(seq_ring, k)]
        if k == 1:
            parts, sent_parts[:] = after((parts, sent_parts))
        if k == 0:
            sent = after(sent_parts[0], tokens)
            come.append([owners.along(part, -s) for s, part in zip(chip_shifts, sent)])
            found["own_other"] = pre_grads(0, 1, [], tokens)
        return parts

    def normed_done(pair):
        pair, come[0] = after((pair, come[0]), found["own_other"])
        return pair

    back_steps = seq_ring.scatter(give_parts, normed_done)
    grad_normed_one = owners.unlist_columns(back_steps)
    done = come[0][0]
    mixture_hop(max(tensor_count // 2 - 2, 1), done)
    sent = after(sent_parts[1], done)
    come.append([owners.along(part, -s) for s, part in zip(chip_shifts, sent)])
    own_other = owners.cross(found["own_other"])
    own_down_grad = down_grads(0, 0, [own_other_down], [done])
    own_pre_grads = pre_grads(0, 0, [own_other], [done])
    for k in range(tensor_count // 2 - 3, 0, -1):
        mixture_hop(k, own_pre_grads)
    layer_out = (residual + mixture_steps.total(mixed[0])).astype(jnp.bfloat16)

    def columns_of(place, seq):
        first = (place * seq_count + seq) * block_width
        return slice(first, first + block_width)

    def summed_piece(p, columns):
        return both_cores(0, pieces[p], columns) + sum(
            part[:, columns].astype(FULL) for part in come[p]
        )

    owned = [[] for _ in range(4)]
    for p in range(2):
        swapped = [
            seq_swap(
                jnp.concatenate(
                    [summed_piece(p, columns_of(place, s)).astype(LOW) for place in range(4)],
                    axis=1,
                ),
                -s,
            )
            for s in seq_shifts
        ]
        for place in range(4):
            columns = slice(place * block_width, (place + 1) * block_width)
            owned[place].append(
                summed_piece(p, columns_of(place, 0))
                + sum(part[:, columns].astype(FULL) for part in swapped)
            )
    owned_query, owned_key, owned_value, owned_out = map(jnp.concatenate, owned)
    owned_out = owned_out.T
    sent_up = [
        owners.along(after(part[1], come[1]), -s) for s, part in zip(chip_shifts, found["pre"])
    ]

    def together(own, *parts):
        return own.astype(FULL) + sum(part.astype(FULL) for part in parts)

    grad_gate = together(own_pre_grads[0], *sent_gate)
    grad_up = together(own_pre_grads[1], *sent_up)
    grad_down = together(own_down_grad, *sent_down)
    def gain_part(grad, place):
        return sum(
            jnp.sum(
                grad[:, m * local_width : (m + 1) * local_width].astype(FULL)
                * mat[place].astype(FULL),
                axis=1,
            )
            for m, mat in enumerate(full_mats)
        )

    listed_norm = jnp.concatenate([gain_part(mine_half, 0), gain_part(own_other_half, 1)])
    grad_norm_gain = owners.unlist_columns(listed_norm[None])[0] / norm_gain

    grad_unit_one = grad_normed_one * norm_gain
    grad_tokens = grad_residual + inv_one * (
        grad_unit_one - unit_one * jnp.mean(grad_unit_one * unit_one, axis=-1, keepdims=True)
    )
    early = lax.psum(
        jnp.concatenate([grad_router, grad_mix_gain[None]]), ("expert", "tensor")
    )
    early = after(early, done)
    late = everywhere(
        after(jnp.concatenate([grad_norm_gain.reshape(-1, head_size), grad_gains]), done)
    )
    return (
        layer_out,
        grad_tokens.astype(jnp.bfloat16),
        late[:-2].reshape(-1),
        owned_query,
        owned_key,
        owned_value,
        late[-2],
        late[-1],
        owned_out,
        early[-1],
        early[:-1].T,
        grad_gate[None],
        grad_up[None],
        grad_down[None],
    )


def solution(mesh):
    in_specs = (
        P(("expert", "tensor"), None),
        P("expert", None),
        P(("expert", "tensor"), None),
        P(),
        P("expert", "tensor"),
        P("expert", "tensor"),
        P("expert", "tensor"),
        P(),
        P(),
        P("tensor", "expert"),
        P(),
        P(),
        P(("expert", "tensor"), None, None),
        P(("expert", "tensor"), None, None),
        P(("expert", "tensor"), None, None),
        P(("expert", "tensor"), None),
    )
    out_specs = (
        P(("expert", "tensor"), None),
        P(("expert", "tensor"), None),
        P(),
        P("expert", "tensor"),
        P("expert", "tensor"),
        P("expert", "tensor"),
        P(),
        P(),
        P("tensor", "expert"),
        P(),
        P(),
        P(("expert", "tensor"), None, None),
        P(("expert", "tensor"), None, None),
        P(("expert", "tensor"), None, None),
    )
    return jax.shard_map(
        per_device, mesh=mesh, in_specs=in_specs, out_specs=out_specs, check_vma=False
    )
```

```python
import functools

import jax
import jax.numpy as jnp
import numpy as np
from jax import lax
from jax.experimental import pallas as pl
from jax.experimental.pallas import tpu as pltpu
from jax.sharding import PartitionSpec as P

WIN = 1024


EPSILON = 1e-05
THETA = 50000.0
MASKED = -1e30
HIGH = lax.Precision.HIGHEST
LOW = jnp.bfloat16
FULL = jnp.float32
ROOM = 58 << 20
ANYWHERE = pl.BlockSpec(memory_space=pl.ANY)
NEAR = pl.BlockSpec(memory_space=pltpu.VMEM)
Shape = jax.ShapeDtypeStruct


def inner_rows(left_side, right_side, precision=None):
    return lax.dot_general(
        left_side,
        right_side,
        (((0,), (0,)), ((), ())),
        precision=precision,
        preferred_element_type=jnp.float32,
    )


def outer_rows(left_side, right_side, precision=None):
    return lax.dot_general(
        left_side,
        right_side,
        (((1,), (1,)), ((), ())),
        precision=precision,
        preferred_element_type=jnp.float32,
    )


def plain_dot(left_side, right_side):
    return jnp.dot(left_side, right_side, preferred_element_type=jnp.float32)


def cost(flops, moved, share):
    return pl.CostEstimate(
        flops=int(flops / share), bytes_accessed=int(moved / share), transcendentals=0
    )


def roomy():
    return pltpu.CompilerParams(vmem_limit_bytes=ROOM)


def fixed_block(shape):
    return pl.BlockSpec(shape, lambda *at: (0,) * len(shape))


def nothing(*refs):
    pass


def after(value, *tokens):
    leaves, tree = jax.tree.flatten(value)
    tokens = jax.tree.leaves(tokens)
    out = pl.pallas_call(
        nothing,
        in_specs=[ANYWHERE] * (len(leaves) + len(tokens)),
        out_specs=[ANYWHERE] * len(leaves),
        out_shape=[Shape(leaf.shape, leaf.dtype) for leaf in leaves],
        input_output_aliases={i: i for i in range(len(leaves))},
        cost_estimate=cost(0, 0, 1),
        name="after",
    )(*leaves, *tokens)
    return jax.tree.unflatten(tree, out)


def fresh_body(value, *refs):
    refs[-1][...] = value[...]


def stack_body(count, *refs):
    for i in range(count):
        pl.when(pl.program_id(0) == i)(functools.partial(fresh_body, refs[i], refs[-1]))


def stack(values, *tokens):
    tokens, count, (rows, columns) = jax.tree.leaves(tokens), len(values), values[0].shape
    return pl.pallas_call(
        functools.partial(stack_body, count),
        grid=(count,),
        in_specs=[fixed_block((rows, columns))] * count + [ANYWHERE] * len(tokens),
        out_specs=pl.BlockSpec((rows, columns), lambda i: (i, 0)),
        out_shape=Shape((count * rows, columns), values[0].dtype),
        compiler_params=roomy(),
        cost_estimate=cost(0, 4 * count * rows * columns, 2),
        name="stack",
    )(*values, *tokens)


def fresh(value, first, rows, *tokens, steps=2):
    tokens = jax.tree.leaves(tokens)
    step = rows // steps
    at = first // step
    return pl.pallas_call(
        fresh_body,
        grid=(steps,),
        in_specs=[pl.BlockSpec((step, value.shape[1]), lambda i: (at + i, 0))]
        + [ANYWHERE] * len(tokens),
        out_specs=pl.BlockSpec((step, value.shape[1]), lambda i: (i, 0)),
        out_shape=Shape((rows, value.shape[1]), value.dtype),
        compiler_params=roomy(),
        cost_estimate=cost(0, 4 * rows * value.shape[1], 2),
        name="fresh",
    )(value, *tokens)


def experts_body(blocks, experts, slabs, begun, given, ids_at, slabs_at, spots_at, numbers, *refs):
    refs = list(refs)

    def take(count):
        return [refs.pop(0) for _ in range(count)]

    rows_in, cot_in = take(blocks), take(blocks)
    mats = [take(3) for _ in range(slabs)]
    start_rows, start_mixed = take(blocks * begun), take(blocks * begun)
    take(given)
    rows_out, mixed_out, kept_w_out, kept_g_out = take(blocks), take(blocks), *take(2)
    copies = take(0 if begun else 2)
    rows, cot, both, down, rows_sum, mixed_sum, begin, end, kept_w, kept_g, *refs = refs[-15:]
    extra, extra_begin, extra_end, sems, out_sems = refs
    size, hidden, width = rows_in[0].shape[0], down.shape[1], rows.shape[1]
    spans = [pl.ds(b * size, size) for b in range(blocks)]
    spots = [pl.ds(pl.multiple_of(numbers[at], size), size) for at in spots_at]
    loads, stores = [], []

    def load(source, target):
        copy = pltpu.make_async_copy(source, target, sems.at[len(loads)])
        copy.start()
        loads.append(copy)
        return copy

    def store(source, target):
        copy = pltpu.make_async_copy(source, target, out_sems.at[len(stores)])
        copy.start()
        stores.append(copy)

    main, rest = pl.ds(0, width), pl.ds(width, extra.shape[1])
    rows_loads = [load(rows_in[b].at[:, main], rows.at[spans[b]]) for b in range(blocks)]
    extra_loads = [load(rows_in[b].at[:, rest], extra.at[spans[b]]) for b in range(blocks)]
    if begun:
        extra_loads += [
            load(start_rows[b].at[:, rest], extra_begin.at[spans[b]]) for b in range(blocks)
        ]

    def slab_rows(s, rows, first=0):
        if slabs_at[s] is None:
            return pl.ds(first, rows)
        return pl.ds(pl.multiple_of(numbers[slabs_at[s]] * rows, rows), rows)

    def load_pre(s):
        gate, up, _ = mats[s]
        last = up.shape[0] - width if slabs_at[s] is None else 0
        return [
            load(gate.at[slab_rows(s, width)], both.at[s, :, pl.ds(0, hidden)]),
            load(up.at[slab_rows(s, width, last)], both.at[s, :, pl.ds(hidden, hidden)]),
        ]

    def load_down(s):
        return load(mats[s][2].at[slab_rows(s, hidden)], down.at[s])

    mat_loads = [load_pre(0)]
    cot_loads = [load(cot_in[b], cot.at[spans[b]]) for b in range(blocks)]
    down_loads = [load_down(0)]
    if begun:
        begin_loads = [
            [load(start_rows[b].at[:, main], begin.at[0, spans[b]]) for b in range(blocks)],
            [load(start_mixed[b], begin.at[1, spans[b]]) for b in range(blocks)],
        ]
    for s in range(1, slabs):
        mat_loads.append(load_pre(s))
        down_loads.append(load_down(s))
    for copy in extra_loads:
        copy.wait()
    gates = extra[:, :experts].astype(FULL) + extra[:, experts : 2 * experts].astype(FULL)
    table = extra_begin[:, :experts].astype(FULL) if begun else jnp.zeros(gates.shape, FULL)
    for copy in rows_loads:
        copy.wait()
    for s in range(slabs):
        last = s == slabs - 1
        for copy in mat_loads[s]:
            copy.wait()
        pre = plain_dot(rows[...], both[s])
        if s == 0:
            for copy in cot_loads:
                copy.wait()
            for held, copy_out in zip((rows, cot), copies):
                for b in range(blocks):
                    store(held.at[spans[b]], copy_out.at[spots[b]])
        down_loads[s].wait()
        plain_grad = outer_rows(cot[...], down[s])
        hit = lax.broadcasted_iota(jnp.int32, gates.shape, 1) == numbers[ids_at[s]]
        gate = jnp.sum(jnp.where(hit, gates, 0.0), axis=1, keepdims=True)
        gate_pre, up_pre = pre[:, :hidden], pre[:, hidden:]
        sigmoid_val = 0.5 * jnp.tanh(0.5 * gate_pre) + 0.5
        silu_val = gate_pre * sigmoid_val
        activation = (silu_val * up_pre).astype(LOW).astype(FULL)
        table = table + jnp.where(
            hit, jnp.sum(activation * plain_grad, axis=1, keepdims=True), 0.0
        )
        grad_act = gate * plain_grad
        kept_w[s] = (gate * activation).astype(LOW)
        kept_g[s, :, :hidden] = (
            grad_act * up_pre * (sigmoid_val + silu_val * (1.0 - sigmoid_val))
        ).astype(LOW)
        kept_g[s, :, hidden:] = (grad_act * silu_val).astype(LOW)
        for b in range(blocks):
            store(kept_w.at[s, spans[b]], kept_w_out.at[spots[b], pl.ds(s * hidden, hidden)])
            store(
                kept_g.at[s, spans[b]], kept_g_out.at[spots[b], pl.ds(2 * s * hidden, 2 * hidden)]
            )
        for i, sums in enumerate((rows_sum, mixed_sum)):
            if s == 0 and begun:
                for copy in begin_loads[i]:
                    copy.wait()
            for p in range(2):
                columns = pl.ds(p * (width // 2), width // 2)
                if i == 0:
                    part = outer_rows(kept_g[s], both[s, columns, :])
                else:
                    part = plain_dot(kept_w[s], down[s, :, columns])
                if s > 0:
                    part = part + sums[:, columns]
                elif begun:
                    part = part + begin[i, :, columns].astype(FULL)
                if last:
                    end[i, :, columns] = part.astype(LOW)
                    for b in range(blocks):
                        out = (rows_out, mixed_out)[i][b]
                        store(end.at[i, spans[b], columns], out.at[:, columns])
                else:
                    sums[:, columns] = part
    extra_end[...] = jnp.zeros(extra_end.shape, LOW)
    extra_end[:, :experts] = table.astype(LOW)
    for b in range(blocks):
        store(extra_end.at[spans[b]], rows_out[b].at[:, rest])
    for copy in stores:
        copy.wait()


def experts_call(
    experts,
    numbers,
    ids_at,
    slabs_at,
    spots_at,
    rows,
    cot,
    mats,
    start,
    shared,
    total_rows,
    tokens,
):
    blocks, slabs = len(rows), len(mats)
    size, width = cot[0].shape
    extra = rows[0].shape[1] - width
    hidden, total = mats[0][0].shape[1], blocks * size
    operands = [numbers, *rows, *cot]
    specs = [pl.BlockSpec(memory_space=pltpu.SMEM)] + [ANYWHERE] * (2 * blocks)
    for trio in mats:
        operands += trio
    specs += [ANYWHERE] * (3 * slabs)
    if start is not None:
        operands += [*start[0], *start[1]]
        specs += [ANYWHERE] * (2 * blocks)
    aliases, given = {}, 0
    outs = 2 * blocks
    for j, part in enumerate(shared):
        if part is not None:
            aliases[len(operands)] = outs + j
            operands.append(part)
            specs.append(ANYWHERE)
            given += 1
    given += len(tokens)
    operands += tokens
    specs += [ANYWHERE] * len(tokens)
    wide, hidden_all = Shape((total_rows, width), LOW), slabs * hidden
    out = pl.pallas_call(
        functools.partial(
            experts_body,
            blocks,
            experts,
            slabs,
            int(start is not None),
            given,
            ids_at,
            slabs_at,
            spots_at,
        ),
        in_specs=specs,
        out_specs=[ANYWHERE] * (outs + len(shared)),
        out_shape=[Shape((size, width + extra), LOW)] * blocks
        + [Shape((size, width), LOW)] * blocks
        + [Shape((total_rows, hidden_all), LOW), Shape((total_rows, 2 * hidden_all), LOW)]
        + [wide] * (len(shared) - 2),
        input_output_aliases=aliases,
        scratch_shapes=[
            pltpu.VMEM((total, width), LOW),
            pltpu.VMEM((total, width), LOW),
            pltpu.VMEM((slabs, width, 2 * hidden), LOW),
            pltpu.VMEM((slabs, hidden, width), LOW),
            pltpu.VMEM((total, width), FULL),
            pltpu.VMEM((total, width), FULL),
            pltpu.VMEM((2, total, width), LOW),
            pltpu.VMEM((2, total, width), LOW),
            pltpu.VMEM((slabs, total, hidden), LOW),
            pltpu.VMEM((slabs, total, 2 * hidden), LOW),
            pltpu.VMEM((total, extra), LOW),
            pltpu.VMEM((total, extra), LOW),
            pltpu.VMEM((total, extra), LOW),
            pltpu.SemaphoreType.DMA((6 * blocks + 3 * slabs,)),
            pltpu.SemaphoreType.DMA((2 * slabs * blocks + 7 * blocks,)),
        ],
        compiler_params=roomy(),
        cost_estimate=cost(12 * total * width * hidden * slabs, 0, 2.7),
        name="experts",
    )(*operands)
    return out[:blocks], out[blocks:outs], out[outs:]


def slab_grads_body(swapped, parts, joined, rows, kept, *refs):
    outs = refs[-parts:]
    step, half = pl.program_id(0), pl.num_programs(0) // 2
    total = inner_rows(kept[...], rows[...])
    if swapped:
        total = total.astype(LOW).T.astype(FULL)
    terms, refs = [], list(refs)
    for one in joined:
        if one:
            total = total + refs.pop(0)[...].astype(FULL)
        else:
            terms.append((refs.pop(0), refs.pop(0)))
    if parts == 1:
        outs[0][...] = total.astype(outs[0].dtype)
        return

    def put(part):
        found = total
        for pair in terms:
            found = found + pair[part][...].astype(FULL)
        outs[part][...] = found.astype(outs[part].dtype)

    pl.when(step < half)(functools.partial(put, 0))
    pl.when(step >= half)(functools.partial(put, 1))


def slab_grads_call(rows, kept, first, count, swapped, terms, tokens, parts=1, kind=LOW, step=256):
    total, width = rows.shape
    at, steps = first // step, count // step
    if swapped:
        spec = pl.BlockSpec((width, step), lambda i: (i // steps, i % steps))
        shape = (2 * width, count)
    else:
        spec = pl.BlockSpec((step, width), lambda i: (i, 0))
        shape = (count, width)
    apart = [
        pl.BlockSpec((width, step), lambda i: (0, jnp.minimum(i, steps - 1))),
        pl.BlockSpec((width, step), lambda i: (0, jnp.maximum(i - steps, 0))),
    ]
    out_specs, out_shapes = [spec], [Shape(shape, kind)]
    if parts == 2:
        out_specs, out_shapes = apart, [Shape((width, count), kind)] * 2
    joined = [not isinstance(term, (list, tuple)) for term in terms]
    term_specs = [part for one in joined for part in ([spec] if one else apart)]
    return pl.pallas_call(
        functools.partial(slab_grads_body, swapped, parts, joined),
        grid=((2 if swapped else 1) * steps,),
        in_specs=[
            pl.BlockSpec((total, width), lambda i: (0, 0), pipeline_mode=pl.Buffered(1)),
            pl.BlockSpec((total, step), lambda i: (0, at + i)),
        ]
        + term_specs
        + [ANYWHERE] * len(tokens),
        out_specs=out_specs,
        out_shape=out_shapes,
        compiler_params=roomy(),
        cost_estimate=cost(2 * total * width * count * (2 if swapped else 1), 0, 3),
        name="slab_grads",
    )(rows, kept, *jax.tree.leaves(terms), *tokens)


def rope_tables(length, head_size):
    half_size = head_size // 2
    frequency = THETA ** (-2.0 * np.arange(half_size) / head_size)
    angles = np.arange(length)[:, None] * frequency[None, :]
    cos_part, sin_part = np.cos(angles), np.sin(angles)
    return np.concatenate([cos_part, cos_part, -sin_part, sin_part], axis=1).astype(np.float32)


def half_turn(vectors):
    return pltpu.roll(vectors, vectors.shape[1] // 2, 1)


def project_body(rows, query, query_rest, key, key_rest, gains, tables, *refs):
    query_proj, query_low, key_proj, key_low = refs[-4:]
    half = query.shape[0]

    def both_halves(mat, rest):
        return plain_dot(rows[:, :half], mat[...]) + plain_dot(rows[:, half:], rest[...])

    size = gains.shape[1]
    cos_two, sin_two = tables[:, :size], tables[:, size:]
    for mat, rest, gain, proj_out, low_out in (
        (query, query_rest, gains[0:1], query_proj, query_low),
        (key, key_rest, gains[1:2], key_proj, key_low),
    ):
        proj = both_halves(mat, rest)
        proj_out[...] = proj
        for h in range(mat.shape[1] // size):
            columns = slice(h * size, (h + 1) * size)
            head = proj[:, columns]
            head = head * lax.rsqrt(jnp.mean(head * head, axis=-1, keepdims=True) + EPSILON)
            head = head * gain
            low_out[:, columns] = (head * cos_two + half_turn(head) * sin_two).astype(LOW)


def project_call(rows, mats, gains, tables, tokens):
    total, width = rows.shape
    mats = [half for halves in mats for half in halves]
    columns, step = mats[0].shape[1], min(256, total)
    row_block = pl.BlockSpec((step, columns), lambda i: (i, 0))
    full, low = Shape((total, columns), FULL), Shape((total, columns), LOW)
    return pl.pallas_call(
        project_body,
        grid=(total // step,),
        in_specs=[pl.BlockSpec((step, width), lambda i: (i, 0))]
        + [fixed_block(mat.shape) for mat in mats]
        + [fixed_block(gains.shape), pl.BlockSpec((step, tables.shape[1]), lambda i: (i, 0))]
        + [ANYWHERE] * len(tokens),
        out_specs=[row_block] * 4,
        out_shape=[full, low, full, low],
        compiler_params=roomy(),
        cost_estimate=cost(4 * total * width * columns, 0, 2),
        name="project",
    )(rows, *mats, gains, tables, *tokens)


def value_body(rows, mat, rest, *refs):
    half = mat.shape[0]
    refs[-1][...] = (
        plain_dot(rows[:, :half], mat[...]) + plain_dot(rows[:, half:], rest[...])
    ).astype(LOW)


def value_call(rows, mat, rest, tokens):
    total, width = rows.shape
    columns, step = mat.shape[1], min(256, total)
    return pl.pallas_call(
        value_body,
        grid=(total // step,),
        in_specs=[
            pl.BlockSpec((step, width), lambda i: (i, 0)),
            fixed_block(mat.shape),
            fixed_block(rest.shape),
        ]
        + [ANYWHERE] * len(tokens),
        out_specs=pl.BlockSpec((step, columns), lambda i: (i, 0)),
        out_shape=Shape((total, columns), LOW),
        compiler_params=roomy(),
        cost_estimate=cost(2 * total * width * columns, 0, 2),
        name="values",
    )(rows, mat, rest, *tokens)


def held_pairs(seg_col, seg_row, pos_col, pos_row):
    same = seg_col == seg_row
    if seg_row.shape[1] > WIN:
        same = same & (jnp.abs(pos_col - pos_row) < WIN)
    return same


def softmax_rows(query, key, held):
    scores = outer_rows(query, key) * (query.shape[1] ** -0.5)
    scores = jnp.where(held, scores, MASKED)
    raised = jnp.exp(scores - jnp.max(scores, axis=-1, keepdims=True))
    return raised * (1.0 / jnp.sum(raised, axis=-1, keepdims=True))


def attend_body(query, key, value, seg_col, seg_row, pos_col, pos_row, *refs):
    out = refs[-1]
    held = held_pairs(seg_col[...], seg_row[...], pos_col[...], pos_row[...])
    probs = softmax_rows(query[...], key[...], held).astype(LOW)
    out[...] = plain_dot(probs, value[...]).astype(LOW)


def attend_call(query, key, value, places, size, first, rows, tokens):
    total, columns = query.shape
    heads = columns // size
    at = first // rows
    column_block = pl.BlockSpec((total, size), lambda h: (0, h))
    col = pl.BlockSpec((rows, 1), lambda h: (at, 0))
    row = fixed_block((1, total))
    return pl.pallas_call(
        attend_body,
        grid=(heads,),
        in_specs=[
            pl.BlockSpec((rows, size), lambda h: (at, h)),
            column_block,
            column_block,
            col,
            row,
            col,
            row,
        ]
        + [ANYWHERE] * len(tokens),
        out_specs=pl.BlockSpec((rows, size), lambda h: (0, h)),
        out_shape=Shape((rows, columns), LOW),
        compiler_params=roomy(),
        cost_estimate=cost(4 * rows * total * columns, 0, 0.5),
        name="attend",
    )(query, key, value, *places, *tokens)


def unprepare(grad, proj, gain, cos_two, sin_two):
    inverse = lax.rsqrt(jnp.mean(proj * proj, axis=-1, keepdims=True) + EPSILON)
    unit = proj * inverse
    grad = grad * cos_two + half_turn(grad * sin_two)
    gain_grad = jnp.sum(grad * unit, axis=0, keepdims=True)
    grad = grad * gain
    return inverse * (grad - unit * jnp.mean(grad * unit, axis=-1, keepdims=True)), gain_grad


def attend_back_body(
    step,
    query,
    key,
    value,
    grad,
    query_proj,
    key_proj,
    gains,
    tables,
    seg_col,
    seg_row,
    pos_col,
    pos_row,
    grad_query,
    grad_key,
    grad_value,
    grad_gains,
    query_sum,
    key_sum,
    value_sum,
):
    total, size = query.shape
    scaling = size**-0.5
    for q in range(total // step):
        at = pl.ds(q * step, step)
        held = held_pairs(seg_col[at], seg_row[...], pos_col[at], pos_row[...])
        probs = softmax_rows(query[at], key[...], held)
        grad_probs = outer_rows(grad[at], value[...]).astype(LOW).astype(FULL)
        weighted = probs * grad_probs
        centre = jnp.sum(weighted, axis=-1, keepdims=True)
        grad_scores = (weighted - probs * centre).astype(LOW)
        query_sum[at] = plain_dot(grad_scores, key[...]) * scaling
        key_part = inner_rows(grad_scores, query[at])
        value_part = inner_rows(probs.astype(LOW), grad[at])
        if q == 0:
            key_sum[...] = key_part
            value_sum[...] = value_part
        else:
            key_sum[...] += key_part
            value_sum[...] += value_part
    grad_value[...] = value_sum[...].astype(LOW)
    turns = (tables[:, :size], tables[:, size:])
    query_part, query_gain_part = unprepare(
        query_sum[...], query_proj[...], gains[0:1], *turns
    )
    key_part, key_gain_part = unprepare(
        key_sum[...] * scaling, key_proj[...], gains[1:2], *turns
    )
    grad_query[...] = query_part.astype(LOW)
    grad_key[...] = key_part.astype(LOW)

    @pl.when(pl.program_id(0) == 0)
    def _():
        grad_gains[...] = jnp.zeros_like(grad_gains)

    grad_gains[0:1] += query_gain_part
    grad_gains[1:2] += key_gain_part


def attend_back_call(
    query, key, value, grad, query_proj, key_proj, gains, tables, places, tokens
):
    total, columns = query.shape
    size = gains.shape[1]
    heads, step = columns // size, min(256, total)
    head = pl.BlockSpec((total, size), lambda h: (0, h))
    fixed = (gains, tables, *places)
    return pl.pallas_call(
        lambda *refs: attend_back_body(
            step, *refs[: 6 + len(fixed)], *refs[6 + len(fixed) + len(tokens) :]
        ),
        grid=(heads,),
        in_specs=[head] * 6
        + [fixed_block(a.shape) for a in fixed]
        + [ANYWHERE] * len(tokens),
        out_specs=[head] * 3 + [fixed_block((2, size))],
        out_shape=[Shape((total, columns), LOW)] * 3 + [Shape((2, size), FULL)],
        scratch_shapes=[pltpu.VMEM((total, size), FULL)] * 3,
        compiler_params=roomy(),
        cost_estimate=cost(10 * total * total * columns, 0, 5),
        name="attend_back",
    )(query, key, value, grad, query_proj, key_proj, *fixed, *tokens)


def attended_back_body(count, mat, *refs):
    out = refs[-1]
    size = refs[0].shape[0]
    for b in range(count):
        out[b * size : (b + 1) * size] = outer_rows(refs[b][...], mat[...]).astype(LOW)


def attended_back_call(blocks, mat, given, first, total):
    size, width = blocks[0].shape
    columns, count = mat.shape[0], len(blocks)
    at = first // (count * size)
    given = [] if given is None else [given]
    return pl.pallas_call(
        functools.partial(attended_back_body, count),
        grid=(1,),
        in_specs=[fixed_block((columns, width))]
        + [fixed_block((size, width))] * count
        + [ANYWHERE] * len(given),
        out_specs=pl.BlockSpec((count * size, columns), lambda i: (at, 0)),
        out_shape=Shape((total, columns), LOW),
        input_output_aliases={1 + count: 0} if given else {},
        compiler_params=roomy(),
        cost_estimate=cost(2 * count * size * width * columns, 0, 10),
        name="attended_back",
    )(mat, *blocks, *given)


def rows_back_body(count, *refs):
    grads, firsts, rests = (refs[k * count : (k + 1) * count] for k in range(3))
    outs = refs[3 * count :]
    step, steps, size = pl.program_id(0), pl.num_programs(0), outs[0].shape[0]

    def run(mats):
        total = outer_rows(grads[0][...], mats[0][...])
        for grad, mat in zip(grads[1:], mats[1:]):
            total = total + outer_rows(grad[...], mat[...])
        for b, out in enumerate(outs):
            out[...] = total[b * size : (b + 1) * size].astype(LOW)

    pl.when(step < steps // 2)(lambda: run(firsts))
    pl.when(step >= steps // 2)(lambda: run(rests))


def rows_back_call(grads, mats, size, tokens):
    (rows, columns), count = grads[0].shape, len(grads)
    half, blocks = mats[0][0].shape[0], rows // size
    step = half // 2

    def body(*refs):
        rows_back_body(count, *refs[: 3 * count], *refs[3 * count + len(tokens) :])

    return pl.pallas_call(
        body,
        grid=(4,),
        in_specs=[fixed_block((rows, columns))] * count
        + [pl.BlockSpec((step, columns), lambda i: (jnp.minimum(i, 1), 0))] * count
        + [pl.BlockSpec((step, columns), lambda i: (jnp.maximum(i - 2, 0), 0))] * count
        + [ANYWHERE] * len(tokens),
        out_specs=[pl.BlockSpec((size, step), lambda i: (0, i))] * blocks,
        out_shape=[Shape((size, 2 * half), LOW)] * blocks,
        compiler_params=roomy(),
        cost_estimate=cost(4 * count * rows * columns * half, 0, 2.5),
        name="rows_back",
    )(*grads, *[mat[0] for mat in mats], *[mat[1] for mat in mats], *tokens)


def weight_back_body(columns, count, rows, query, key, value, *refs):
    branch, attended, out = refs[:count], refs[count : 2 * count], refs[-1]
    for place, right in enumerate((query, key, value)):
        out[:, place * columns : (place + 1) * columns] = inner_rows(
            rows[...], right[...]
        ).astype(LOW)
    out[:, 3 * columns :] = sum(
        inner_rows(left[...], right[...]) for left, right in zip(branch, attended)
    ).astype(LOW)


def weight_back_call(rows, branch, grads, attended, half, tokens, step=512):
    (total, width), (size, columns), count = rows.shape, attended[0].shape, len(branch)
    steps = width // 2 // step

    def part(height):
        return pl.BlockSpec((height, step), lambda i: (0, half * steps + i))

    return pl.pallas_call(
        lambda *refs: weight_back_body(
            columns, count, *refs[: 4 + 2 * count], refs[-1]
        ),
        grid=(steps,),
        in_specs=[part(total)]
        + [fixed_block((total, columns))] * 3
        + [part(size)] * count
        + [fixed_block((size, columns))] * count
        + [ANYWHERE] * len(tokens),
        out_specs=pl.BlockSpec((step, 4 * columns), lambda i: (i, 0)),
        out_shape=Shape((width // 2, 4 * columns), LOW),
        compiler_params=roomy(),
        cost_estimate=cost(4 * total * width * columns, 0, 2.5),
        name="weight_back",
    )(rows, *grads, *branch, *attended, *tokens)


def gain_body(columns, others, mine, *refs):
    mats, out = refs[:6], refs[-1]
    half = mine.shape[0]
    for place, grads in enumerate((mine, others)):
        out[place * half : (place + 1) * half] = sum(
            jnp.sum(
                grads[:, m * columns : (m + 1) * columns].astype(FULL)
                * mats[2 * m + place][...].astype(FULL),
                axis=1,
                keepdims=True,
            )
            for m in range(3)
        )


def gain_call(others, mine, mats, columns, tokens):
    half = mine.shape[0]
    part = fixed_block((half, 3 * columns))
    return pl.pallas_call(
        functools.partial(gain_body, columns),
        grid=(1,),
        in_specs=[part, part]
        + [fixed_block((half, columns))] * 6
        + [ANYWHERE] * len(tokens),
        out_specs=fixed_block((2 * half, 1)),
        out_shape=Shape((2 * half, 1), FULL),
        compiler_params=roomy(),
        cost_estimate=cost(0, 12 * half * columns, 2),
        name="gain",
    )(others, mine, *mats, *tokens)


class Ring:
    def __init__(self, axis, size, count):
        self.axis, self.count = axis, count
        self.order = list(range(0, count, 2)) + list(range(count - 1, 0, -2))
        self.rightward = [
            (base + self.order[k], base + self.order[(k + 1) % count])
            for base in range(0, size, count)
            for k in range(count)
        ]
        self.leftward = [(to, start) for start, to in self.rightward]

    def right(self, value):
        return jax.tree.map(lambda v: lax.ppermute(v, self.axis, self.rightward), value)

    def left(self, value):
        return jax.tree.map(lambda v: lax.ppermute(v, self.axis, self.leftward), value)

    def members(self, at):
        count = self.count
        spot = jnp.where(at % 2 == 0, at // 2, count - (at + 1) // 2)
        shifts = [0]
        for k in range(1, count // 2):
            shifts += [-k, k]
        shifts.append(count // 2)
        spots = [(spot + shift + count) % count for shift in shifts]
        return [jnp.where(p < count // 2, 2 * p, 2 * (count - p) - 1) for p in spots]

    def gather(self, value, use, between):
        from_left = from_right = value
        use(0, [value])
        for k in range(1, self.count // 2):
            from_left, from_right = between(k, (self.right(from_left), self.left(from_right)))
            use(k, [from_left, from_right])
        upper = self.right(jax.tree.map(lambda v: v[: v.shape[0] // 2], from_left))
        lower = self.left(jax.tree.map(lambda v: v[v.shape[0] // 2 :], from_right))
        upper, lower = between(self.count // 2, (upper, lower))
        use(
            self.count // 2,
            [jax.tree.map(lambda u, v: jnp.concatenate([u, v]), upper, lower)],
        )

    def scatter(self, make, finish=lambda pair: pair):
        steps = Reduction(self)
        tokens = []
        for k in range(self.count // 2, 0, -1):
            tokens = steps.hop(make(k, tokens))
        (own,) = make(0, tokens)
        steps.pair = finish(steps.pair)
        return steps.total(own)


class Spread:
    def __init__(self, ring, value):
        self.ring, self.pair, self.blocks, self.hops = ring, (value, value), [value], 0
        self.settled = True

    def hop(self, *tokens):
        ring = self.ring
        if not self.settled:
            self.settle(*tokens)
        left, right = self.pair
        self.hops, self.settled = self.hops + 1, False
        if self.hops == ring.count // 2:
            left, right = left[: left.shape[0] // 2], right[right.shape[0] // 2 :]
        self.pair = (ring.right(left), ring.left(right))

    def settle(self, *tokens):
        self.pair, self.settled = after(self.pair, *tokens), True
        if self.hops == self.ring.count // 2:
            self.blocks.append(jnp.concatenate(self.pair))
        else:
            self.blocks.extend(self.pair)


class Reduction:
    def __init__(self, ring):
        self.ring, self.pair = ring, None

    def hop(self, terms, *tokens):
        ring = self.ring
        if self.pair is None:
            (far,) = terms
            if tokens:
                far = after(far, *tokens)
            half = far.shape[0] // 2
            sent = [far]
            self.pair = (ring.right(far[:half]), ring.left(far[half:]))
        else:
            on_left, on_right = terms
            from_left, from_right = self.pair
            half = from_left.shape[0]
            if half < on_left.shape[0]:
                to_right = jnp.concatenate([on_right[:half] + from_left, on_right[half:]])
                to_left = jnp.concatenate([on_left[:half], on_left[half:] + from_right])
            else:
                to_right, to_left = on_right + from_left, on_left + from_right
            sent = [to_right, to_left]
            if tokens:
                sent = after(sent, *tokens)
            self.pair = (ring.right(sent[0]), ring.left(sent[1]))
        self.sent = sent
        return sent

    def total(self, own):
        return own.astype(FULL) + self.pair[0].astype(FULL) + self.pair[1].astype(FULL)


class Owners:
    def __init__(self):
        self.count = lax.axis_size("expert")
        self.chips = self.count // 2
        self.here = lax.axis_index("expert")

    def cross(self, value):
        pairs = [(i, i ^ 1) for i in range(self.count)]
        return jax.tree.map(lambda v: lax.ppermute(v, "expert", pairs), value)

    def along(self, value, shift):
        pairs = [(i, (i + 2 * shift) % self.count) for i in range(self.count)]
        return jax.tree.map(lambda v: lax.ppermute(v, "expert", pairs), value)

    def over_cores(self, value):
        groups = [[2 * i, 2 * i + 1] for i in range(self.chips)]
        return lax.all_gather(value, "expert", axis_index_groups=groups, axis=0, tiled=True)

    def from_core(self, value):
        rows = value.shape[0]
        at = (self.here + 1) % 2 * rows
        return lax.dynamic_slice_in_dim(self.over_cores(value), at, rows, 0)

    def over_chips(self, value, shift):
        groups = [[2 * i + core for i in range(self.chips)] for core in range(2)]
        found = lax.all_gather(value, "expert", axis_index_groups=groups, axis=0, tiled=True)
        rows = value.shape[0]
        at = (self.here // 2 + shift) % self.chips
        return lax.dynamic_slice_in_dim(found, at * rows, rows, 0)

    def listed(self):
        chip, core = self.here // 2, self.here % 2
        return [
            (chip - shift + self.chips) % self.chips * 2 + (core ^ other)
            for other in range(2)
            for shift in range(self.chips)
        ]

    def places(self):
        chip, core = self.here // 2, self.here % 2
        return [
            (core ^ (at % 2)) * self.chips + (chip - at // 2 + self.chips) % self.chips
            for at in range(self.count)
        ]

    def scatter(self, parts):
        mine, other = parts[: self.chips], parts[self.chips :]
        other = self.cross(jnp.concatenate(other, axis=0))
        rows = mine[0].shape[0]
        total = None
        for shift in reversed(range(self.chips)):
            part = mine[shift].astype(FULL) + other[shift * rows : (shift + 1) * rows].astype(FULL)
            if shift:
                part = self.along(part.astype(LOW), -shift).astype(FULL)
            total = part if total is None else total + part
        return total

    def pick_columns(self, rows, places):
        size = rows.shape[1] // self.count
        return jnp.concatenate(
            [lax.dynamic_slice_in_dim(rows, at * size, size, 1) for at in places], axis=1
        )

    def list_columns(self, rows):
        return self.pick_columns(rows, self.listed())

    def unlist_columns(self, rows):
        return self.pick_columns(rows, self.places())


class Everywhere:
    def __init__(self, value):
        self.value, self.own, self.hops = None, value, []
        for axis in ("expert", "tensor"):
            size, step = lax.axis_size(axis), 1
            while step < size:
                self.hops.append((axis, [(i, i ^ step) for i in range(size)]))
                step *= 2
        self.hops = [self.hops[0], self.hops[-1], *self.hops[1:-1]]

    def hop(self):
        if self.value is not None:
            self.own, self.value = self.own + self.value, None
        if self.hops:
            self.value = lax.ppermute(self.own, *self.hops.pop(0))


def per_device(
    tokens,
    segments,
    routes,
    norm_gain,
    w_query,
    w_key,
    w_value,
    query_gain,
    key_gain,
    w_out,
    mix_gain,
    w_router,
    w_gate,
    w_up,
    w_down,
    cotangent,
):
    tensor_count = lax.axis_size("tensor")
    expert_count = w_router.shape[1]
    tok_rows, model_width = tokens.shape
    seq_count, length = segments.shape
    head_size = query_gain.shape[0]
    part_count = tensor_count // seq_count
    block_width = w_query.shape[1]
    local_width = seq_count * block_width
    tensor_at = lax.axis_index("tensor")
    seq_at, part_at = tensor_at // part_count, tensor_at % part_count
    whole_ring = Ring("tensor", tensor_count, tensor_count)
    seq_ring = Ring("tensor", tensor_count, part_count)
    owners = Owners()

    def seq_swap(value, shift):
        pairs = [(t, (t + part_count * shift) % tensor_count) for t in range(tensor_count)]
        return lax.ppermute(value, "tensor", pairs)

    inputs = tokens.astype(jnp.float32)
    inv_one = lax.rsqrt(jnp.mean(inputs * inputs, axis=-1, keepdims=True) + EPSILON)
    unit_one = inputs * inv_one
    normed_one = owners.list_columns((unit_one * norm_gain).astype(jnp.bfloat16))

    seq_shifts, chip_shifts = range(1, seq_count), range(1, owners.chips)
    hidden, total_rows = w_down.shape[1], tensor_count * tok_rows
    own_slab = (w_gate[0], w_up[0], w_down[0])
    copies = [
        fresh(cotangent, 0, tok_rows, normed_one),
        stack(own_slab[:2], normed_one),
        fresh(own_slab[2], 0, hidden, normed_one),
        fresh(w_value, 0, w_value.shape[0], normed_one),
        fresh(w_out, 0, w_out.shape[0], normed_one),
    ]
    both_slabs = [owners.over_cores(w) for w in own_slab]
    query_key = jnp.concatenate([w_query, w_key], axis=1)
    gathered, found = [], {}
    wave = [seq_swap(query_key, s) for s in seq_shifts]

    def between(k, pair):
        nonlocal wave
        if k == 1:
            pair, moved, copies[:] = after((pair, wave, copies))
            heads = [query_key, *moved]
            found["pair"] = jnp.concatenate(
                [h[:, :block_width] for h in heads] + [h[:, block_width:] for h in heads], axis=1
            )
            wave = [
                *[owners.along(found["pair"], s) for s in chip_shifts],
                *[seq_swap(w, s) for s in seq_shifts for w in copies[3:]],
            ]
        elif k == part_count // 2:
            pair, moved = after((pair, wave))
            count = owners.chips - 1
            found["pair"] = jnp.concatenate([found["pair"], *moved[:count]], axis=0)
            found["value"] = jnp.concatenate([w_value, *moved[count::2]], axis=1)
            found["out"] = jnp.concatenate([w_out, *moved[count + 1 :: 2]], axis=0)
            wave = [owners.along(found[w], s) for w in ("value", "out") for s in chip_shifts]
            found["token"] = moved
        return pair

    seq_ring.gather(normed_one, lambda k, blocks: gathered.extend(blocks), between)
    normed_all = jnp.concatenate(gathered)
    own_cot, own_both, own_down = copies[:3]
    pair_rest = owners.cross(found["pair"])
    cot_steps = Spread(whole_ring, after(own_cot, pair_rest))
    cot_steps.hop()
    pair_mats = [
        (found["pair"][:, :local_width], pair_rest[:, :local_width]),
        (found["pair"][:, local_width:], pair_rest[:, local_width:]),
    ]

    whole_members = whole_ring.members(tensor_at)
    seq_members = seq_ring.members(part_at)
    numbers = jnp.stack(
        [at * tok_rows for at in whole_members]
        + [(at * tensor_count + tensor_at) // 2 for at in owners.listed()]
        + [(owners.here + 1) % 2]
    )
    ids_from = tensor_count

    def from_place(table):
        return jnp.concatenate(
            [
                lax.dynamic_slice_in_dim(table, at * tok_rows, tok_rows, 0)
                for at in seq_members
            ]
        )

    tables = from_place(jnp.array(rope_tables(length, head_size)))
    seg_row = lax.dynamic_index_in_dim(segments, seq_at, 0, keepdims=False)
    marks = from_place(jnp.stack([seg_row, jnp.arange(length, dtype=jnp.int32)], axis=1))
    places = (marks[:, :1], marks[:, :1].T, marks[:, 1:], marks[:, 1:].T)
    gains = jnp.stack([query_gain, key_gain])

    query_proj, query_low, key_proj, key_low = project_call(
        normed_all, pair_mats, gains, tables, []
    )
    wave = after(wave, query_low)
    count = owners.chips - 1
    found["value"] = jnp.concatenate([found["value"], *wave[:count]], axis=0)
    found["out"] = jnp.concatenate([found["out"], *wave[count:]], axis=1)
    value_rest, out_rest = owners.cross((found["value"], found["out"]))
    full_mats = [*pair_mats, (found["value"], value_rest)]
    cot_steps.hop(query_low)
    value_low = value_call(normed_all, found["value"], value_rest, cot_steps.blocks[1:])
    out_full = jnp.concatenate([found["out"], out_rest], axis=1)
    far_down = [owners.along(after(own_down, wave), s) for s in chip_shifts]

    def place_of(ring, k):
        return {0: [0], ring.count // 2: [ring.count - 1]}.get(k, [2 * k - 1, 2 * k])

    far_both = []
    attended = [None] * part_count

    def branch_parts(k, tokens):
        parts, tokens = [], list(tokens)
        if k == 0:
            tokens += far_down
            far_both.extend(owners.along(after(own_both, *far_down), s) for s in chip_shifts)
        for b in place_of(seq_ring, k):
            attended[b] = attend_call(
                query_low,
                key_low,
                value_low,
                places,
                head_size,
                b * tok_rows,
                tok_rows,
                tokens,
            )
            parts.append(plain_dot(attended[b], out_full).astype(LOW))
        if k == 1:
            cot_steps.settle(parts)
            parts = after(parts, cot_steps.pair)
        return parts

    branch = seq_ring.scatter(branch_parts)
    cot_steps.pair = after(cot_steps.pair, branch)
    cot_steps.hop()
    residual = inputs + owners.unlist_columns(branch)
    inv_two = lax.rsqrt(jnp.mean(residual * residual, axis=-1, keepdims=True) + EPSILON)
    unit_two = residual * inv_two
    normed_two = (unit_two * mix_gain).astype(jnp.bfloat16)
    logits = jnp.dot(normed_two, w_router, preferred_element_type=jnp.float32)
    hits = jnp.any(
        routes[:, :, None] == jnp.arange(expert_count, dtype=jnp.int32)[None, None, :], axis=1
    )
    top_logit = jnp.max(jnp.where(hits, logits, MASKED), axis=-1, keepdims=True)
    raised = jnp.where(hits, jnp.exp(logits - top_logit), 0.0)
    gate_table = raised / jnp.sum(raised, axis=-1, keepdims=True)

    grad_out = cotangent.astype(jnp.float32)
    slab_mats = {0: [own_slab, both_slabs]}
    row_blocks, sums, mixed = ([None] * tensor_count for _ in range(3))
    shared_all = []

    def run_experts(shift, k, tokens):
        at = place_of(whole_ring, k)
        if len(shared_all) == shift:
            shared_all.append([None] * (2 if shift else 4))
        parts, mixed_parts, shared_all[shift] = experts_call(
            expert_count,
            numbers,
            [ids_from + shift, ids_from + owners.chips + shift],
            [None, None if shift else ids_from + owners.count],
            at,
            [row_blocks[b] for b in at],
            [cot_steps.blocks[b] for b in at],
            slab_mats[shift],
            [[part[b] for b in at] for part in (sums, mixed)] if shift else None,
            shared_all[shift],
            total_rows,
            tokens,
        )
        for b, part, mixed_part in zip(at, parts, mixed_parts):
            sums[b], mixed[b] = part, mixed_part
        return [sums[b] for b in at]

    def first_pair(k, blocks):
        for b, rows in zip(place_of(whole_ring, k), blocks):
            row_blocks[b] = rows
        run_experts(0, k, [])

    def next_hop(k, pair):
        done = [sums[b] for b in place_of(whole_ring, k - 1)]
        if k == 1:
            pair, cot_steps.pair = after((pair, cot_steps.pair), *done)
            while cot_steps.hops < tensor_count // 2:
                cot_steps.hop()
        elif k == 2:
            pair, cot_steps.pair = after((pair, cot_steps.pair), *done)
            cot_steps.settle()
            far_down[:] = after(far_down, pair)
            found["down"] = owners.cross(far_down)
        elif k == tensor_count // 2 - 1:
            pair, far_both[:], found["down"] = after((pair, far_both, found["down"]), *done)
        elif k < tensor_count // 2:
            pair = after(pair, *done)
        return pair

    high = lax.reduce_precision(gate_table, 8, 7)
    room = -2 * expert_count % 128
    payload = jnp.concatenate(
        [
            normed_two,
            high.astype(LOW),
            (gate_table - high).astype(LOW),
            jnp.zeros((tok_rows, room), LOW),
        ],
        axis=1,
    )
    whole_ring.gather(payload, first_pair, next_hop)
    far_other = owners.cross(far_both)
    for i, shift in enumerate(chip_shifts):
        slab_mats[shift] = [
            (far_both[i], far_both[i], far_down[i]),
            (far_other[i], far_other[i], found["down"][i]),
        ]
    for shift in range(1, owners.chips - 1):
        for k in range(tensor_count // 2 + 1):
            run_experts(shift, k, [])

    def last_pair(k, tokens):
        return run_experts(owners.chips - 1, k, jax.tree.leaves(tokens))

    def down_grads(shift, other, terms, tokens):
        kept, all_cot = shared_all[shift][0], shared_all[0][3]
        return slab_grads_call(all_cot, kept, other * hidden, hidden, False, terms, tokens)[0]

    def pre_grads(shift, other, terms, tokens):
        kept, rows = shared_all[shift][1], shared_all[0][2]
        return slab_grads_call(rows, kept, 2 * other * hidden, hidden, True, terms, tokens)[0]

    def finish(pair):
        others = [down_grads(s, 1, [], [sums[0]]) for s in chip_shifts]
        pair, others = after((pair, others))
        found["down"] = owners.cross(others)
        return pair

    summed_rows = whole_ring.scatter(last_pair, finish)
    grad_rows_sum = summed_rows[:, :model_width]
    grad_gates = summed_rows[:, model_width : model_width + expert_count]

    grad_logits = gate_table * (
        grad_gates - jnp.sum(gate_table * grad_gates, axis=-1, keepdims=True)
    )
    grad_normed_two = grad_rows_sum + outer_rows(grad_logits, w_router.astype(jnp.float32), HIGH)
    grad_router = inner_rows(grad_logits, normed_two.astype(jnp.float32), HIGH)
    grad_unit_two = grad_normed_two * mix_gain
    grad_mix_gain = jnp.sum(grad_normed_two * unit_two, axis=0)
    grad_residual = grad_out + inv_two * (
        grad_unit_two - unit_two * jnp.mean(grad_unit_two * unit_two, axis=-1, keepdims=True)
    )
    grad_branch = owners.list_columns(grad_residual.astype(jnp.bfloat16))
    gathered_back, sent_down = [], []
    mixture_steps = Reduction(whole_ring)

    def back_hop(k, pair):
        if k == 1:
            down = [
                down_grads(s, 0, [other], [grad_branch])
                for s, other in zip(chip_shifts, found["down"])
            ]
            sent_down.extend(owners.along(part, -s) for s, part in zip(chip_shifts, down))
            others = [pre_grads(s, 1, [], down) for s in chip_shifts]
            pair, others = after((pair, others))
            mixture_steps.hop(mixed[-1:], pair[0])
            others = [owners.cross(other) for other in others]
            found["attn"] = None
            for b, block in enumerate([*gathered_back, *pair]):
                found["attn"] = attended_back_call(
                    [block], out_full, found["attn"], b * tok_rows, length
                )
            found["pre"] = [
                pre_grads(s, 0, [other], [found["attn"]]) for s, other in zip(chip_shifts, others)
            ]
        elif k == part_count // 2:
            pair, mixture_steps.pair = after((pair, mixture_steps.pair), found["pre"])
        return pair

    seq_ring.gather(grad_branch, lambda k, blocks: gathered_back.extend(blocks), back_hop)
    grad_attn = found["attn"]
    for b in range(3, part_count):
        grad_attn = attended_back_call(
            [gathered_back[b]], out_full, grad_attn, b * tok_rows, length
        )

    def mixture_hop(k, *tokens):
        mixture_steps.hop([mixed[b] for b in place_of(whole_ring, k)], *tokens)

    mixture_steps.pair, sent_down[:] = after((mixture_steps.pair, sent_down), grad_attn)
    mixture_hop(tensor_count // 2 - 1)
    sent_pre = [
        owners.along(after(part, sent_down), -s) for s, part in zip(chip_shifts, found["pre"])
    ]
    *head_grads, grad_gains = attend_back_call(
        query_low,
        key_low,
        value_low,
        grad_attn,
        query_proj,
        key_proj,
        gains,
        tables,
        places,
        list(mixture_steps.sent),
    )

    own_other_half = weight_back_call(
        normed_all,
        gathered_back,
        head_grads,
        attended,
        1,
        list(mixture_steps.pair),
    )
    other_half = owners.cross(own_other_half)
    mine_half = weight_back_call(
        normed_all, gathered_back, head_grads, attended, 0, [own_other_half]
    )
    mixture_steps.pair = after(mixture_steps.pair, own_other_half)
    mixture_hop(max(tensor_count // 2 - 2, 1))
    normed_parts = rows_back_call(
        head_grads, full_mats, tok_rows, [mine_half, *mixture_steps.sent]
    )
    listed_norm = gain_call(
        own_other_half,
        mine_half,
        [m for pair in full_mats for m in pair],
        local_width,
        [normed_parts[-1], *mixture_steps.pair, *sent_pre],
    )
    grad_norm_gain = owners.unlist_columns(listed_norm.T) / norm_gain
    room = model_width - grad_gains.size
    small_steps = Everywhere(
        jnp.concatenate(
            [
                grad_router,
                grad_mix_gain[None],
                grad_norm_gain,
                jnp.pad(grad_gains.reshape(1, -1), ((0, 0), (0, room))),
            ]
        )
    )
    small_steps.hop()
    chip_rows = model_width // owners.count
    piece_rows = chip_rows // 2
    pieces = [slice(p * piece_rows, (p + 1) * piece_rows) for p in range(2)]

    def both_cores(shift, rows, columns=slice(None)):
        rows = slice(shift * chip_rows + rows.start, shift * chip_rows + rows.stop)
        return mine_half[rows, columns].astype(FULL) + other_half[rows, columns].astype(FULL)

    sent_parts = [[both_cores(s, rows).astype(LOW) for s in chip_shifts] for rows in pieces]
    come = []

    def give_parts(k, tokens):
        parts = [normed_parts[b] for b in place_of(seq_ring, k)]
        if k == 1:
            parts, sent_parts[:], small_steps.value = after(
                (parts, sent_parts, small_steps.value)
            )
            small_steps.hop()
        if k == 0:
            sent = after(sent_parts[0], tokens)
            come.append([owners.along(part, -s) for s, part in zip(chip_shifts, sent)])
            found["own_other_down"] = down_grads(0, 1, [], tokens)
            found["own_other"] = pre_grads(0, 1, [], [found["own_other_down"]])
        return parts

    def normed_done(pair):
        pair, come[0], small_steps.value = after(
            (pair, come[0], small_steps.value), found["own_other"]
        )
        small_steps.hop()
        return pair

    grad_normed_one = seq_ring.scatter(give_parts, normed_done)
    done = grad_normed_one
    grad_normed_one = owners.unlist_columns(grad_normed_one)
    sent = after(sent_parts[1], done)
    come.append([owners.along(part, -s) for s, part in zip(chip_shifts, sent)])
    mixture_steps.pair = after(mixture_steps.pair, done)
    for k in range(tensor_count // 2 - 3, 0, -1):
        mixture_hop(k)
    own_other_down, own_other = owners.cross(
        after((found["own_other_down"], found["own_other"]), done)
    )
    (grad_down,) = slab_grads_call(
        shared_all[0][3],
        shared_all[0][0],
        0,
        hidden,
        False,
        [own_other_down, *sent_down],
        [done],
        kind=FULL,
    )
    come[1], small_steps.value = after((come[1], small_steps.value), grad_down)
    small_steps.hop()
    grad_gate, grad_up = slab_grads_call(
        shared_all[0][2],
        shared_all[0][1],
        0,
        hidden,
        True,
        [own_other, *sent_pre],
        come[1],
        parts=2,
        kind=FULL,
    )
    def columns_of(place, seq):
        first = (place * seq_count + seq) * block_width
        return slice(first, first + block_width)

    def summed_piece(p, columns):
        return both_cores(0, pieces[p], columns) + sum(
            part[:, columns].astype(FULL) for part in come[p]
        )

    swapped_pieces = [
        [
            seq_swap(
                jnp.concatenate(
                    [summed_piece(p, columns_of(place, s)).astype(LOW) for place in range(4)],
                    axis=1,
                ),
                -s,
            )
            for s in seq_shifts
        ]
        for p in range(2)
    ]
    mixture_steps.pair, small_steps.value = after(
        (mixture_steps.pair, small_steps.value), grad_gate
    )
    layer_out = (residual + mixture_steps.total(mixed[0])).astype(jnp.bfloat16)
    grad_unit_one = grad_normed_one * norm_gain
    grad_tokens = grad_residual + inv_one * (
        grad_unit_one - unit_one * jnp.mean(grad_unit_one * unit_one, axis=-1, keepdims=True)
    )
    grad_tokens = grad_tokens.astype(jnp.bfloat16)
    swapped_pieces = after(swapped_pieces, layer_out, grad_tokens)
    owned = [[] for _ in range(4)]
    for p, swapped in enumerate(swapped_pieces):
        for place in range(4):
            columns = slice(place * block_width, (place + 1) * block_width)
            owned[place].append(
                summed_piece(p, columns_of(place, 0))
                + sum(part[:, columns].astype(FULL) for part in swapped)
            )
    owned_query, owned_key, owned_value, owned_out = map(jnp.concatenate, owned)
    owned_out = owned_out.T
    while small_steps.value is not None:
        small_steps.hop()
    small = small_steps.own
    small_gains = small[-1, : grad_gains.size].reshape(grad_gains.shape)
    return (
        layer_out,
        grad_tokens,
        small[-2],
        owned_query,
        owned_key,
        owned_value,
        small_gains[0],
        small_gains[1],
        owned_out,
        small[-3],
        small[:-3].T,
        grad_gate[None],
        grad_up[None],
        grad_down[None],
    )


def solution(mesh):
    in_specs = (
        P(("expert", "tensor"), None),
        P("expert", None),
        P(("expert", "tensor"), None),
        P(),
        P("expert", "tensor"),
        P("expert", "tensor"),
        P("expert", "tensor"),
        P(),
        P(),
        P("tensor", "expert"),
        P(),
        P(),
        P(("expert", "tensor"), None, None),
        P(("expert", "tensor"), None, None),
        P(("expert", "tensor"), None, None),
        P(("expert", "tensor"), None),
    )
    out_specs = (
        P(("expert", "tensor"), None),
        P(("expert", "tensor"), None),
        P(),
        P("expert", "tensor"),
        P("expert", "tensor"),
        P("expert", "tensor"),
        P(),
        P(),
        P("tensor", "expert"),
        P(),
        P(),
        P(("expert", "tensor"), None, None),
        P(("expert", "tensor"), None, None),
        P(("expert", "tensor"), None, None),
    )
    return jax.shard_map(
        per_device, mesh=mesh, in_specs=in_specs, out_specs=out_specs, check_vma=False
    )
```

```python
import functools

import jax
import jax.numpy as jnp
import numpy as np
from jax import lax
from jax.experimental import pallas as pl
from jax.experimental.pallas import tpu as pltpu
from jax.sharding import PartitionSpec as P

WIN = 1024


EPSILON = 1e-05
THETA = 50000.0
MASKED = -1e30
HIGH = lax.Precision.HIGHEST
LOW = jnp.bfloat16
FULL = jnp.float32
ROOM = 58 << 20
ANYWHERE = pl.BlockSpec(memory_space=pl.ANY)
NEAR = pl.BlockSpec(memory_space=pltpu.VMEM)
Shape = jax.ShapeDtypeStruct


def inner_rows(left_side, right_side, precision=None):
    return lax.dot_general(
        left_side,
        right_side,
        (((0,), (0,)), ((), ())),
        precision=precision,
        preferred_element_type=jnp.float32,
    )


def outer_rows(left_side, right_side, precision=None):
    return lax.dot_general(
        left_side,
        right_side,
        (((1,), (1,)), ((), ())),
        precision=precision,
        preferred_element_type=jnp.float32,
    )


def plain_dot(left_side, right_side):
    return jnp.dot(left_side, right_side, preferred_element_type=jnp.float32)


def cost(flops, moved, share):
    return pl.CostEstimate(
        flops=int(flops / share), bytes_accessed=int(moved / share), transcendentals=0
    )


def roomy():
    return pltpu.CompilerParams(vmem_limit_bytes=ROOM)


def fixed_block(shape):
    return pl.BlockSpec(shape, lambda *at: (0,) * len(shape))


def nothing(*refs):
    pass


def after(value, *tokens):
    leaves, tree = jax.tree.flatten(value)
    tokens = jax.tree.leaves(tokens)
    out = pl.pallas_call(
        nothing,
        in_specs=[ANYWHERE] * (len(leaves) + len(tokens)),
        out_specs=[ANYWHERE] * len(leaves),
        out_shape=[Shape(leaf.shape, leaf.dtype) for leaf in leaves],
        input_output_aliases={i: i for i in range(len(leaves))},
        cost_estimate=cost(0, 0, 1),
        name="after",
    )(*leaves, *tokens)
    return jax.tree.unflatten(tree, out)


def fresh_body(value, *refs):
    refs[-1][...] = value[...]


def stack_body(count, *refs):
    for i in range(count):
        pl.when(pl.program_id(0) == i)(functools.partial(fresh_body, refs[i], refs[-1]))


def stack(values, *tokens):
    tokens, count, (rows, columns) = jax.tree.leaves(tokens), len(values), values[0].shape
    return pl.pallas_call(
        functools.partial(stack_body, count),
        grid=(count,),
        in_specs=[fixed_block((rows, columns))] * count + [ANYWHERE] * len(tokens),
        out_specs=pl.BlockSpec((rows, columns), lambda i: (i, 0)),
        out_shape=Shape((count * rows, columns), values[0].dtype),
        compiler_params=roomy(),
        cost_estimate=cost(0, 4 * count * rows * columns, 2),
        name="stack",
    )(*values, *tokens)


def fresh(value, first, rows, *tokens, steps=2):
    tokens = jax.tree.leaves(tokens)
    step = rows // steps
    at = first // step
    return pl.pallas_call(
        fresh_body,
        grid=(steps,),
        in_specs=[pl.BlockSpec((step, value.shape[1]), lambda i: (at + i, 0))]
        + [ANYWHERE] * len(tokens),
        out_specs=pl.BlockSpec((step, value.shape[1]), lambda i: (i, 0)),
        out_shape=Shape((rows, value.shape[1]), value.dtype),
        compiler_params=roomy(),
        cost_estimate=cost(0, 4 * rows * value.shape[1], 2),
        name="fresh",
    )(value, *tokens)


def experts_body(blocks, experts, slabs, begun, given, ids_at, slabs_at, spots_at, numbers, *refs):
    refs = list(refs)

    def take(count):
        return [refs.pop(0) for _ in range(count)]

    rows_in, cot_in = take(blocks), take(blocks)
    mats = [take(3) for _ in range(slabs)]
    start_rows, start_mixed = take(blocks * begun), take(blocks * begun)
    take(given)
    rows_out, mixed_out, kept_w_out, kept_g_out = take(blocks), take(blocks), *take(2)
    copies = take(0 if begun else 2)
    rows, cot, both, down, rows_sum, mixed_sum, begin, end, kept_w, kept_g, *refs = refs[-15:]
    extra, extra_begin, extra_end, sems, out_sems = refs
    size, hidden, width = rows_in[0].shape[0], down.shape[1], rows.shape[1]
    spans = [pl.ds(b * size, size) for b in range(blocks)]
    spots = [pl.ds(pl.multiple_of(numbers[at], size), size) for at in spots_at]
    loads, stores = [], []

    def load(source, target):
        copy = pltpu.make_async_copy(source, target, sems.at[len(loads)])
        copy.start()
        loads.append(copy)
        return copy

    def store(source, target):
        copy = pltpu.make_async_copy(source, target, out_sems.at[len(stores)])
        copy.start()
        stores.append(copy)

    main, rest = pl.ds(0, width), pl.ds(width, extra.shape[1])
    rows_loads = [load(rows_in[b].at[:, main], rows.at[spans[b]]) for b in range(blocks)]
    extra_loads = [load(rows_in[b].at[:, rest], extra.at[spans[b]]) for b in range(blocks)]
    if begun:
        extra_loads += [
            load(start_rows[b].at[:, rest], extra_begin.at[spans[b]]) for b in range(blocks)
        ]

    def slab_rows(s, rows, first=0):
        if slabs_at[s] is None:
            return pl.ds(first, rows)
        return pl.ds(pl.multiple_of(numbers[slabs_at[s]] * rows, rows), rows)

    def load_pre(s):
        gate, up, _ = mats[s]
        last = up.shape[0] - width if slabs_at[s] is None else 0
        return [
            load(gate.at[slab_rows(s, width)], both.at[s, :, pl.ds(0, hidden)]),
            load(up.at[slab_rows(s, width, last)], both.at[s, :, pl.ds(hidden, hidden)]),
        ]

    def load_down(s):
        return load(mats[s][2].at[slab_rows(s, hidden)], down.at[s])

    mat_loads = [load_pre(0)]
    cot_loads = [load(cot_in[b], cot.at[spans[b]]) for b in range(blocks)]
    down_loads = [load_down(0)]
    if begun:
        begin_loads = [
            [load(start_rows[b].at[:, main], begin.at[0, spans[b]]) for b in range(blocks)],
            [load(start_mixed[b], begin.at[1, spans[b]]) for b in range(blocks)],
        ]
    for s in range(1, slabs):
        mat_loads.append(load_pre(s))
        down_loads.append(load_down(s))
    for copy in extra_loads:
        copy.wait()
    gates = extra[:, :experts].astype(FULL) + extra[:, experts : 2 * experts].astype(FULL)
    table = extra_begin[:, :experts].astype(FULL) if begun else jnp.zeros(gates.shape, FULL)
    for copy in rows_loads:
        copy.wait()
    for s in range(slabs):
        last = s == slabs - 1
        for copy in mat_loads[s]:
            copy.wait()
        pre = plain_dot(rows[...], both[s])
        if s == 0:
            for copy in cot_loads:
                copy.wait()
            for held, copy_out in zip((rows, cot), copies):
                for b in range(blocks):
                    store(held.at[spans[b]], copy_out.at[spots[b]])
        down_loads[s].wait()
        plain_grad = outer_rows(cot[...], down[s])
        hit = lax.broadcasted_iota(jnp.int32, gates.shape, 1) == numbers[ids_at[s]]
        gate = jnp.sum(jnp.where(hit, gates, 0.0), axis=1, keepdims=True)
        gate_pre, up_pre = pre[:, :hidden], pre[:, hidden:]
        sigmoid_val = 0.5 * jnp.tanh(0.5 * gate_pre) + 0.5
        silu_val = gate_pre * sigmoid_val
        activation = (silu_val * up_pre).astype(LOW).astype(FULL)
        table = table + jnp.where(
            hit, jnp.sum(activation * plain_grad, axis=1, keepdims=True), 0.0
        )
        grad_act = gate * plain_grad
        kept_w[s] = (gate * activation).astype(LOW)
        kept_g[s, :, :hidden] = (
            grad_act * up_pre * (sigmoid_val + silu_val * (1.0 - sigmoid_val))
        ).astype(LOW)
        kept_g[s, :, hidden:] = (grad_act * silu_val).astype(LOW)
        for b in range(blocks):
            store(kept_w.at[s, spans[b]], kept_w_out.at[spots[b], pl.ds(s * hidden, hidden)])
            store(
                kept_g.at[s, spans[b]], kept_g_out.at[spots[b], pl.ds(2 * s * hidden, 2 * hidden)]
            )
        for i, sums in enumerate((rows_sum, mixed_sum)):
            if s == 0 and begun:
                for copy in begin_loads[i]:
                    copy.wait()
            for p in range(2):
                columns = pl.ds(p * (width // 2), width // 2)
                if i == 0:
                    part = outer_rows(kept_g[s], both[s, columns, :])
                else:
                    part = plain_dot(kept_w[s], down[s, :, columns])
                if s > 0:
                    part = part + sums[:, columns]
                elif begun:
                    part = part + begin[i, :, columns].astype(FULL)
                if last:
                    end[i, :, columns] = part.astype(LOW)
                    for b in range(blocks):
                        out = (rows_out, mixed_out)[i][b]
                        store(end.at[i, spans[b], columns], out.at[:, columns])
                else:
                    sums[:, columns] = part
    extra_end[...] = jnp.zeros(extra_end.shape, LOW)
    extra_end[:, :experts] = table.astype(LOW)
    for b in range(blocks):
        store(extra_end.at[spans[b]], rows_out[b].at[:, rest])
    for copy in stores:
        copy.wait()


def experts_call(
    experts,
    numbers,
    ids_at,
    slabs_at,
    spots_at,
    rows,
    cot,
    mats,
    start,
    shared,
    total_rows,
    tokens,
):
    blocks, slabs = len(rows), len(mats)
    size, width = cot[0].shape
    extra = rows[0].shape[1] - width
    hidden, total = mats[0][0].shape[1], blocks * size
    operands = [numbers, *rows, *cot]
    specs = [pl.BlockSpec(memory_space=pltpu.SMEM)] + [ANYWHERE] * (2 * blocks)
    for trio in mats:
        operands += trio
    specs += [ANYWHERE] * (3 * slabs)
    if start is not None:
        operands += [*start[0], *start[1]]
        specs += [ANYWHERE] * (2 * blocks)
    aliases, given = {}, 0
    outs = 2 * blocks
    for j, part in enumerate(shared):
        if part is not None:
            aliases[len(operands)] = outs + j
            operands.append(part)
            specs.append(ANYWHERE)
            given += 1
    given += len(tokens)
    operands += tokens
    specs += [ANYWHERE] * len(tokens)
    wide, hidden_all = Shape((total_rows, width), LOW), slabs * hidden
    out = pl.pallas_call(
        functools.partial(
            experts_body,
            blocks,
            experts,
            slabs,
            int(start is not None),
            given,
            ids_at,
            slabs_at,
            spots_at,
        ),
        in_specs=specs,
        out_specs=[ANYWHERE] * (outs + len(shared)),
        out_shape=[Shape((size, width + extra), LOW)] * blocks
        + [Shape((size, width), LOW)] * blocks
        + [Shape((total_rows, hidden_all), LOW), Shape((total_rows, 2 * hidden_all), LOW)]
        + [wide] * (len(shared) - 2),
        input_output_aliases=aliases,
        scratch_shapes=[
            pltpu.VMEM((total, width), LOW),
            pltpu.VMEM((total, width), LOW),
            pltpu.VMEM((slabs, width, 2 * hidden), LOW),
            pltpu.VMEM((slabs, hidden, width), LOW),
            pltpu.VMEM((total, width), FULL),
            pltpu.VMEM((total, width), FULL),
            pltpu.VMEM((2, total, width), LOW),
            pltpu.VMEM((2, total, width), LOW),
            pltpu.VMEM((slabs, total, hidden), LOW),
            pltpu.VMEM((slabs, total, 2 * hidden), LOW),
            pltpu.VMEM((total, extra), LOW),
            pltpu.VMEM((total, extra), LOW),
            pltpu.VMEM((total, extra), LOW),
            pltpu.SemaphoreType.DMA((6 * blocks + 3 * slabs,)),
            pltpu.SemaphoreType.DMA((2 * slabs * blocks + 7 * blocks,)),
        ],
        compiler_params=roomy(),
        cost_estimate=cost(12 * total * width * hidden * slabs, 0, 2.7),
        name="experts",
    )(*operands)
    return out[:blocks], out[blocks:outs], out[outs:]


def slab_grads_body(swapped, parts, joined, rows, kept, *refs):
    outs = refs[-parts:]
    step, half = pl.program_id(0), pl.num_programs(0) // 2
    total = inner_rows(kept[...], rows[...])
    if swapped:
        total = total.astype(LOW).T.astype(FULL)
    terms, refs = [], list(refs)
    for one in joined:
        if one:
            total = total + refs.pop(0)[...].astype(FULL)
        else:
            terms.append((refs.pop(0), refs.pop(0)))
    if parts == 1:
        outs[0][...] = total.astype(outs[0].dtype)
        return

    def put(part):
        found = total
        for pair in terms:
            found = found + pair[part][...].astype(FULL)
        outs[part][...] = found.astype(outs[part].dtype)

    pl.when(step < half)(functools.partial(put, 0))
    pl.when(step >= half)(functools.partial(put, 1))


def slab_grads_call(rows, kept, first, count, swapped, terms, tokens, parts=1, kind=LOW, step=256):
    total, width = rows.shape
    at, steps = first // step, count // step
    if swapped:
        spec = pl.BlockSpec((width, step), lambda i: (i // steps, i % steps))
        shape = (2 * width, count)
    else:
        spec = pl.BlockSpec((step, width), lambda i: (i, 0))
        shape = (count, width)
    apart = [
        pl.BlockSpec((width, step), lambda i: (0, jnp.minimum(i, steps - 1))),
        pl.BlockSpec((width, step), lambda i: (0, jnp.maximum(i - steps, 0))),
    ]
    out_specs, out_shapes = [spec], [Shape(shape, kind)]
    if parts == 2:
        out_specs, out_shapes = apart, [Shape((width, count), kind)] * 2
    joined = [not isinstance(term, (list, tuple)) for term in terms]
    term_specs = [part for one in joined for part in ([spec] if one else apart)]
    return pl.pallas_call(
        functools.partial(slab_grads_body, swapped, parts, joined),
        grid=((2 if swapped else 1) * steps,),
        in_specs=[
            pl.BlockSpec((total, width), lambda i: (0, 0), pipeline_mode=pl.Buffered(1)),
            pl.BlockSpec((total, step), lambda i: (0, at + i)),
        ]
        + term_specs
        + [ANYWHERE] * len(tokens),
        out_specs=out_specs,
        out_shape=out_shapes,
        compiler_params=roomy(),
        cost_estimate=cost(2 * total * width * count * (2 if swapped else 1), 0, 3),
        name="slab_grads",
    )(rows, kept, *jax.tree.leaves(terms), *tokens)


def rope_tables(length, head_size):
    half_size = head_size // 2
    frequency = THETA ** (-2.0 * np.arange(half_size) / head_size)
    angles = np.arange(length)[:, None] * frequency[None, :]
    cos_part, sin_part = np.cos(angles), np.sin(angles)
    return np.concatenate([cos_part, cos_part, -sin_part, sin_part], axis=1).astype(np.float32)


def half_turn(vectors):
    return pltpu.roll(vectors, vectors.shape[1] // 2, 1)


def project_body(rows, query, query_rest, key, key_rest, gains, tables, *refs):
    query_proj, query_low, key_proj, key_low = refs[-4:]
    half = query.shape[0]

    def both_halves(mat, rest):
        return plain_dot(rows[:, :half], mat[...]) + plain_dot(rows[:, half:], rest[...])

    size = gains.shape[1]
    cos_two, sin_two = tables[:, :size], tables[:, size:]
    for mat, rest, gain, proj_out, low_out in (
        (query, query_rest, gains[0:1], query_proj, query_low),
        (key, key_rest, gains[1:2], key_proj, key_low),
    ):
        proj = both_halves(mat, rest)
        proj_out[...] = proj
        for h in range(mat.shape[1] // size):
            columns = slice(h * size, (h + 1) * size)
            head = proj[:, columns]
            head = head * lax.rsqrt(jnp.mean(head * head, axis=-1, keepdims=True) + EPSILON)
            head = head * gain
            low_out[:, columns] = (head * cos_two + half_turn(head) * sin_two).astype(LOW)


def project_call(rows, mats, gains, tables, tokens):
    total, width = rows.shape
    mats = [half for halves in mats for half in halves]
    columns, step = mats[0].shape[1], min(256, total)
    row_block = pl.BlockSpec((step, columns), lambda i: (i, 0))
    full, low = Shape((total, columns), FULL), Shape((total, columns), LOW)
    return pl.pallas_call(
        project_body,
        grid=(total // step,),
        in_specs=[pl.BlockSpec((step, width), lambda i: (i, 0))]
        + [fixed_block(mat.shape) for mat in mats]
        + [fixed_block(gains.shape), pl.BlockSpec((step, tables.shape[1]), lambda i: (i, 0))]
        + [ANYWHERE] * len(tokens),
        out_specs=[row_block] * 4,
        out_shape=[full, low, full, low],
        compiler_params=roomy(),
        cost_estimate=cost(4 * total * width * columns, 0, 2),
        name="project",
    )(rows, *mats, gains, tables, *tokens)


def value_body(rows, mat, rest, *refs):
    half = mat.shape[0]
    refs[-1][...] = (
        plain_dot(rows[:, :half], mat[...]) + plain_dot(rows[:, half:], rest[...])
    ).astype(LOW)


def value_call(rows, mat, rest, tokens):
    total, width = rows.shape
    columns, step = mat.shape[1], min(256, total)
    return pl.pallas_call(
        value_body,
        grid=(total // step,),
        in_specs=[
            pl.BlockSpec((step, width), lambda i: (i, 0)),
            fixed_block(mat.shape),
            fixed_block(rest.shape),
        ]
        + [ANYWHERE] * len(tokens),
        out_specs=pl.BlockSpec((step, columns), lambda i: (i, 0)),
        out_shape=Shape((total, columns), LOW),
        compiler_params=roomy(),
        cost_estimate=cost(2 * total * width * columns, 0, 2),
        name="values",
    )(rows, mat, rest, *tokens)


def held_pairs(seg_col, seg_row, pos_col, pos_row):
    same = seg_col == seg_row
    if seg_row.shape[1] > WIN:
        same = same & (jnp.abs(pos_col - pos_row) < WIN)
    return same


def softmax_rows(query, key, held):
    scores = outer_rows(query, key) * (query.shape[1] ** -0.5)
    scores = jnp.where(held, scores, MASKED)
    raised = jnp.exp(scores - jnp.max(scores, axis=-1, keepdims=True))
    return raised * (1.0 / jnp.sum(raised, axis=-1, keepdims=True))


def attend_body(query, key, value, seg_col, seg_row, pos_col, pos_row, *refs):
    out = refs[-1]
    held = held_pairs(seg_col[...], seg_row[...], pos_col[...], pos_row[...])
    probs = softmax_rows(query[...], key[...], held).astype(LOW)
    out[...] = plain_dot(probs, value[...]).astype(LOW)


def attend_call(query, key, value, places, size, first, rows, tokens):
    total, columns = query.shape
    heads = columns // size
    at = first // rows
    column_block = pl.BlockSpec((total, size), lambda h: (0, h))
    col = pl.BlockSpec((rows, 1), lambda h: (at, 0))
    row = fixed_block((1, total))
    return pl.pallas_call(
        attend_body,
        grid=(heads,),
        in_specs=[
            pl.BlockSpec((rows, size), lambda h: (at, h)),
            column_block,
            column_block,
            col,
            row,
            col,
            row,
        ]
        + [ANYWHERE] * len(tokens),
        out_specs=pl.BlockSpec((rows, size), lambda h: (0, h)),
        out_shape=Shape((rows, columns), LOW),
        compiler_params=roomy(),
        cost_estimate=cost(4 * rows * total * columns, 0, 0.5),
        name="attend",
    )(query, key, value, *places, *tokens)


def unprepare(grad, proj, gain, cos_two, sin_two):
    inverse = lax.rsqrt(jnp.mean(proj * proj, axis=-1, keepdims=True) + EPSILON)
    unit = proj * inverse
    grad = grad * cos_two + half_turn(grad * sin_two)
    gain_grad = jnp.sum(grad * unit, axis=0, keepdims=True)
    grad = grad * gain
    return inverse * (grad - unit * jnp.mean(grad * unit, axis=-1, keepdims=True)), gain_grad


def attend_back_body(
    step,
    query,
    key,
    value,
    grad,
    query_proj,
    key_proj,
    gains,
    tables,
    seg_col,
    seg_row,
    pos_col,
    pos_row,
    grad_query,
    grad_key,
    grad_value,
    grad_gains,
    query_sum,
    key_sum,
    value_sum,
):
    total, size = query.shape
    scaling = size**-0.5
    for q in range(total // step):
        at = pl.ds(q * step, step)
        held = held_pairs(seg_col[at], seg_row[...], pos_col[at], pos_row[...])
        probs = softmax_rows(query[at], key[...], held)
        grad_probs = outer_rows(grad[at], value[...]).astype(LOW).astype(FULL)
        weighted = probs * grad_probs
        centre = jnp.sum(weighted, axis=-1, keepdims=True)
        grad_scores = (weighted - probs * centre).astype(LOW)
        query_sum[at] = plain_dot(grad_scores, key[...]) * scaling
        key_part = inner_rows(grad_scores, query[at])
        value_part = inner_rows(probs.astype(LOW), grad[at])
        if q == 0:
            key_sum[...] = key_part
            value_sum[...] = value_part
        else:
            key_sum[...] += key_part
            value_sum[...] += value_part
    grad_value[...] = value_sum[...].astype(LOW)
    turns = (tables[:, :size], tables[:, size:])
    query_part, query_gain_part = unprepare(
        query_sum[...], query_proj[...], gains[0:1], *turns
    )
    key_part, key_gain_part = unprepare(
        key_sum[...] * scaling, key_proj[...], gains[1:2], *turns
    )
    grad_query[...] = query_part.astype(LOW)
    grad_key[...] = key_part.astype(LOW)

    @pl.when(pl.program_id(0) == 0)
    def _():
        grad_gains[...] = jnp.zeros_like(grad_gains)

    grad_gains[0:1] += query_gain_part
    grad_gains[1:2] += key_gain_part


def attend_back_call(
    query, key, value, grad, query_proj, key_proj, gains, tables, places, tokens
):
    total, columns = query.shape
    size = gains.shape[1]
    heads, step = columns // size, min(256, total)
    head = pl.BlockSpec((total, size), lambda h: (0, h))
    fixed = (gains, tables, *places)
    return pl.pallas_call(
        lambda *refs: attend_back_body(
            step, *refs[: 6 + len(fixed)], *refs[6 + len(fixed) + len(tokens) :]
        ),
        grid=(heads,),
        in_specs=[head] * 6
        + [fixed_block(a.shape) for a in fixed]
        + [ANYWHERE] * len(tokens),
        out_specs=[head] * 3 + [fixed_block((2, size))],
        out_shape=[Shape((total, columns), LOW)] * 3 + [Shape((2, size), FULL)],
        scratch_shapes=[pltpu.VMEM((total, size), FULL)] * 3,
        compiler_params=roomy(),
        cost_estimate=cost(10 * total * total * columns, 0, 5),
        name="attend_back",
    )(query, key, value, grad, query_proj, key_proj, *fixed, *tokens)


def attended_back_body(count, mat, *refs):
    out = refs[-1]
    size = refs[0].shape[0]
    for b in range(count):
        out[b * size : (b + 1) * size] = outer_rows(refs[b][...], mat[...]).astype(LOW)


def attended_back_call(blocks, mat, given, first, total, tokens):
    size, width = blocks[0].shape
    columns, count = mat.shape[0], len(blocks)
    at = first // (count * size)
    given = [] if given is None else [given]
    return pl.pallas_call(
        functools.partial(attended_back_body, count),
        grid=(1,),
        in_specs=[fixed_block((columns, width))]
        + [fixed_block((size, width))] * count
        + [ANYWHERE] * (len(given) + len(tokens)),
        out_specs=pl.BlockSpec((count * size, columns), lambda i: (at, 0)),
        out_shape=Shape((total, columns), LOW),
        input_output_aliases={1 + count: 0} if given else {},
        compiler_params=roomy(),
        cost_estimate=cost(2 * count * size * width * columns, 0, 10),
        name="attended_back",
    )(mat, *blocks, *given, *tokens)


def rows_back_body(count, *refs):
    grads, firsts, rests = (refs[k * count : (k + 1) * count] for k in range(3))
    outs = refs[3 * count :]
    step, steps, size = pl.program_id(0), pl.num_programs(0), outs[0].shape[0]

    def run(mats):
        total = outer_rows(grads[0][...], mats[0][...])
        for grad, mat in zip(grads[1:], mats[1:]):
            total = total + outer_rows(grad[...], mat[...])
        for b, out in enumerate(outs):
            out[...] = total[b * size : (b + 1) * size].astype(LOW)

    pl.when(step < steps // 2)(lambda: run(firsts))
    pl.when(step >= steps // 2)(lambda: run(rests))


def rows_back_call(grads, mats, size, tokens):
    (rows, columns), count = grads[0].shape, len(grads)
    half, blocks = mats[0][0].shape[0], rows // size
    step = half // 2

    def body(*refs):
        rows_back_body(count, *refs[: 3 * count], *refs[3 * count + len(tokens) :])

    return pl.pallas_call(
        body,
        grid=(4,),
        in_specs=[fixed_block((rows, columns))] * count
        + [pl.BlockSpec((step, columns), lambda i: (jnp.minimum(i, 1), 0))] * count
        + [pl.BlockSpec((step, columns), lambda i: (jnp.maximum(i - 2, 0), 0))] * count
        + [ANYWHERE] * len(tokens),
        out_specs=[pl.BlockSpec((size, step), lambda i: (0, i))] * blocks,
        out_shape=[Shape((size, 2 * half), LOW)] * blocks,
        compiler_params=roomy(),
        cost_estimate=cost(4 * count * rows * columns * half, 0, 25),
        name="rows_back",
    )(*grads, *[mat[0] for mat in mats], *[mat[1] for mat in mats], *tokens)


def weight_back_body(columns, count, rows, query, key, value, *refs):
    branch, attended, out = refs[:count], refs[count : 2 * count], refs[-1]
    for place, right in enumerate((query, key, value)):
        out[:, place * columns : (place + 1) * columns] = inner_rows(
            rows[...], right[...]
        ).astype(LOW)
    out[:, 3 * columns :] = sum(
        inner_rows(left[...], right[...]) for left, right in zip(branch, attended)
    ).astype(LOW)


def weight_back_call(rows, branch, grads, attended, half, tokens, step=512):
    (total, width), (size, columns), count = rows.shape, attended[0].shape, len(branch)
    steps = width // 2 // step

    def part(height):
        return pl.BlockSpec((height, step), lambda i: (0, half * steps + i))

    return pl.pallas_call(
        lambda *refs: weight_back_body(
            columns, count, *refs[: 4 + 2 * count], refs[-1]
        ),
        grid=(steps,),
        in_specs=[part(total)]
        + [fixed_block((total, columns))] * 3
        + [part(size)] * count
        + [fixed_block((size, columns))] * count
        + [ANYWHERE] * len(tokens),
        out_specs=pl.BlockSpec((step, 4 * columns), lambda i: (i, 0)),
        out_shape=Shape((width // 2, 4 * columns), LOW),
        compiler_params=roomy(),
        cost_estimate=cost(4 * total * width * columns, 0, 25),
        name="weight_back",
    )(rows, *grads, *branch, *attended, *tokens)


def gain_body(columns, others, mine, *refs):
    mats, out = refs[:6], refs[-1]
    half = mine.shape[0]
    for place, grads in enumerate((mine, others)):
        out[place * half : (place + 1) * half] = sum(
            jnp.sum(
                grads[:, m * columns : (m + 1) * columns].astype(FULL)
                * mats[2 * m + place][...].astype(FULL),
                axis=1,
                keepdims=True,
            )
            for m in range(3)
        )


def gain_call(others, mine, mats, columns, tokens):
    half = mine.shape[0]
    part = fixed_block((half, 3 * columns))
    return pl.pallas_call(
        functools.partial(gain_body, columns),
        grid=(1,),
        in_specs=[part, part]
        + [fixed_block((half, columns))] * 6
        + [ANYWHERE] * len(tokens),
        out_specs=fixed_block((2 * half, 1)),
        out_shape=Shape((2 * half, 1), FULL),
        compiler_params=roomy(),
        cost_estimate=cost(0, 12 * half * columns, 20),
        name="gain",
    )(others, mine, *mats, *tokens)


class Ring:
    def __init__(self, axis, size, count):
        self.axis, self.count = axis, count
        self.order = list(range(0, count, 2)) + list(range(count - 1, 0, -2))
        self.rightward = [
            (base + self.order[k], base + self.order[(k + 1) % count])
            for base in range(0, size, count)
            for k in range(count)
        ]
        self.leftward = [(to, start) for start, to in self.rightward]

    def right(self, value):
        return jax.tree.map(lambda v: lax.ppermute(v, self.axis, self.rightward), value)

    def left(self, value):
        return jax.tree.map(lambda v: lax.ppermute(v, self.axis, self.leftward), value)

    def members(self, at):
        count = self.count
        spot = jnp.where(at % 2 == 0, at // 2, count - (at + 1) // 2)
        shifts = [0]
        for k in range(1, count // 2):
            shifts += [-k, k]
        shifts.append(count // 2)
        spots = [(spot + shift + count) % count for shift in shifts]
        return [jnp.where(p < count // 2, 2 * p, 2 * (count - p) - 1) for p in spots]

    def gather(self, value, use, between):
        from_left = from_right = value
        use(0, [value])
        for k in range(1, self.count // 2):
            from_left, from_right = between(k, (self.right(from_left), self.left(from_right)))
            use(k, [from_left, from_right])
        upper = self.right(jax.tree.map(lambda v: v[: v.shape[0] // 2], from_left))
        lower = self.left(jax.tree.map(lambda v: v[v.shape[0] // 2 :], from_right))
        upper, lower = between(self.count // 2, (upper, lower))
        use(
            self.count // 2,
            [jax.tree.map(lambda u, v: jnp.concatenate([u, v]), upper, lower)],
        )

    def scatter(self, make, finish=lambda pair: pair):
        steps = Reduction(self)
        tokens = []
        for k in range(self.count // 2, 0, -1):
            tokens = steps.hop(make(k, tokens))
        (own,) = make(0, tokens)
        steps.pair = finish(steps.pair)
        return steps.total(own)


class Spread:
    def __init__(self, ring, value):
        self.ring, self.pair, self.blocks, self.hops = ring, (value, value), [value], 0
        self.settled = True

    def hop(self, *tokens):
        ring = self.ring
        if not self.settled:
            self.settle(*tokens)
        left, right = self.pair
        self.hops, self.settled = self.hops + 1, False
        if self.hops == ring.count // 2:
            left, right = left[: left.shape[0] // 2], right[right.shape[0] // 2 :]
        self.pair = (ring.right(left), ring.left(right))

    def settle(self, *tokens):
        self.pair, self.settled = after(self.pair, *tokens), True
        if self.hops == self.ring.count // 2:
            self.blocks.append(jnp.concatenate(self.pair))
        else:
            self.blocks.extend(self.pair)


class Reduction:
    def __init__(self, ring):
        self.ring, self.pair = ring, None

    def hop(self, terms, *tokens):
        ring = self.ring
        if self.pair is None:
            (far,) = terms
            if tokens:
                far = after(far, *tokens)
            half = far.shape[0] // 2
            sent = [far]
            self.pair = (ring.right(far[:half]), ring.left(far[half:]))
        else:
            on_left, on_right = terms
            from_left, from_right = self.pair
            half = from_left.shape[0]
            if half < on_left.shape[0]:
                to_right = jnp.concatenate([on_right[:half] + from_left, on_right[half:]])
                to_left = jnp.concatenate([on_left[:half], on_left[half:] + from_right])
            else:
                to_right, to_left = on_right + from_left, on_left + from_right
            sent = [to_right, to_left]
            if tokens:
                sent = after(sent, *tokens)
            self.pair = (ring.right(sent[0]), ring.left(sent[1]))
        self.sent = sent
        return sent

    def total(self, own):
        return own.astype(FULL) + self.pair[0].astype(FULL) + self.pair[1].astype(FULL)


class Owners:
    def __init__(self):
        self.count = lax.axis_size("expert")
        self.chips = self.count // 2
        self.here = lax.axis_index("expert")

    def cross(self, value):
        pairs = [(i, i ^ 1) for i in range(self.count)]
        return jax.tree.map(lambda v: lax.ppermute(v, "expert", pairs), value)

    def along(self, value, shift):
        pairs = [(i, (i + 2 * shift) % self.count) for i in range(self.count)]
        return jax.tree.map(lambda v: lax.ppermute(v, "expert", pairs), value)

    def over_cores(self, value):
        groups = [[2 * i, 2 * i + 1] for i in range(self.chips)]
        return lax.all_gather(value, "expert", axis_index_groups=groups, axis=0, tiled=True)

    def from_core(self, value):
        rows = value.shape[0]
        at = (self.here + 1) % 2 * rows
        return lax.dynamic_slice_in_dim(self.over_cores(value), at, rows, 0)

    def over_chips(self, value, shift):
        groups = [[2 * i + core for i in range(self.chips)] for core in range(2)]
        found = lax.all_gather(value, "expert", axis_index_groups=groups, axis=0, tiled=True)
        rows = value.shape[0]
        at = (self.here // 2 + shift) % self.chips
        return lax.dynamic_slice_in_dim(found, at * rows, rows, 0)

    def listed(self):
        chip, core = self.here // 2, self.here % 2
        return [
            (chip - shift + self.chips) % self.chips * 2 + (core ^ other)
            for other in range(2)
            for shift in range(self.chips)
        ]

    def places(self):
        chip, core = self.here // 2, self.here % 2
        return [
            (core ^ (at % 2)) * self.chips + (chip - at // 2 + self.chips) % self.chips
            for at in range(self.count)
        ]

    def scatter(self, parts):
        mine, other = parts[: self.chips], parts[self.chips :]
        other = self.cross(jnp.concatenate(other, axis=0))
        rows = mine[0].shape[0]
        total = None
        for shift in reversed(range(self.chips)):
            part = mine[shift].astype(FULL) + other[shift * rows : (shift + 1) * rows].astype(FULL)
            if shift:
                part = self.along(part.astype(LOW), -shift).astype(FULL)
            total = part if total is None else total + part
        return total

    def pick_columns(self, rows, places):
        size = rows.shape[1] // self.count
        return jnp.concatenate(
            [lax.dynamic_slice_in_dim(rows, at * size, size, 1) for at in places], axis=1
        )

    def list_columns(self, rows):
        return self.pick_columns(rows, self.listed())

    def unlist_columns(self, rows):
        return self.pick_columns(rows, self.places())


class Everywhere:
    def __init__(self, value):
        self.value, self.own, self.hops = None, value, []
        for axis in ("expert", "tensor"):
            size, step = lax.axis_size(axis), 1
            while step < size:
                self.hops.append((axis, [(i, i ^ step) for i in range(size)]))
                step *= 2
        along_tensor = [hop for hop in self.hops[1:] if hop[0] == "tensor"]
        along_expert = [hop for hop in self.hops[1:] if hop[0] == "expert"]
        self.hops = [self.hops[0], *along_tensor[:-1], *along_expert, along_tensor[-1]]

    def hop(self):
        if self.value is not None:
            self.own, self.value = self.own + self.value, None
        if self.hops:
            self.value = lax.ppermute(self.own, *self.hops.pop(0))


def per_device(
    tokens,
    segments,
    routes,
    norm_gain,
    w_query,
    w_key,
    w_value,
    query_gain,
    key_gain,
    w_out,
    mix_gain,
    w_router,
    w_gate,
    w_up,
    w_down,
    cotangent,
):
    tensor_count = lax.axis_size("tensor")
    expert_count = w_router.shape[1]
    tok_rows, model_width = tokens.shape
    seq_count, length = segments.shape
    head_size = query_gain.shape[0]
    part_count = tensor_count // seq_count
    block_width = w_query.shape[1]
    local_width = seq_count * block_width
    tensor_at = lax.axis_index("tensor")
    seq_at, part_at = tensor_at // part_count, tensor_at % part_count
    whole_ring = Ring("tensor", tensor_count, tensor_count)
    seq_ring = Ring("tensor", tensor_count, part_count)
    owners = Owners()

    def seq_swap(value, shift):
        pairs = [(t, (t + part_count * shift) % tensor_count) for t in range(tensor_count)]
        return lax.ppermute(value, "tensor", pairs)

    inputs = tokens.astype(jnp.float32)
    inv_one = lax.rsqrt(jnp.mean(inputs * inputs, axis=-1, keepdims=True) + EPSILON)
    unit_one = inputs * inv_one
    normed_one = owners.list_columns((unit_one * norm_gain).astype(jnp.bfloat16))

    seq_shifts, chip_shifts = range(1, seq_count), range(1, owners.chips)
    hidden, total_rows = w_down.shape[1], tensor_count * tok_rows
    own_slab = (w_gate[0], w_up[0], w_down[0])
    copies = [
        fresh(cotangent, 0, tok_rows, normed_one),
        stack(own_slab[:2], normed_one),
        fresh(own_slab[2], 0, hidden, normed_one),
        fresh(w_value, 0, w_value.shape[0], normed_one),
        fresh(w_out, 0, w_out.shape[0], normed_one),
    ]
    both_slabs = [owners.over_cores(w) for w in own_slab]
    query_key = jnp.concatenate([w_query, w_key], axis=1)
    gathered, found = [], {}
    wave = [seq_swap(query_key, s) for s in seq_shifts]

    def between(k, pair):
        nonlocal wave
        if k == 1:
            pair, moved, copies[:] = after((pair, wave, copies))
            heads = [query_key, *moved]
            found["pair"] = jnp.concatenate(
                [h[:, :block_width] for h in heads] + [h[:, block_width:] for h in heads], axis=1
            )
            wave = [
                *[owners.along(found["pair"], s) for s in chip_shifts],
                *[seq_swap(w, s) for s in seq_shifts for w in copies[3:]],
            ]
        elif k == part_count // 2:
            pair, moved = after((pair, wave))
            count = owners.chips - 1
            found["pair"] = jnp.concatenate([found["pair"], *moved[:count]], axis=0)
            found["value"] = jnp.concatenate([w_value, *moved[count::2]], axis=1)
            found["out"] = jnp.concatenate([w_out, *moved[count + 1 :: 2]], axis=0)
            wave = [owners.along(found[w], s) for w in ("value", "out") for s in chip_shifts]
            found["token"] = moved
        return pair

    seq_ring.gather(normed_one, lambda k, blocks: gathered.extend(blocks), between)
    normed_all = jnp.concatenate(gathered)
    own_cot, own_both, own_down = copies[:3]
    pair_rest = owners.cross(found["pair"])
    cot_steps = Spread(whole_ring, after(own_cot, pair_rest))
    cot_steps.hop()
    pair_mats = [
        (found["pair"][:, :local_width], pair_rest[:, :local_width]),
        (found["pair"][:, local_width:], pair_rest[:, local_width:]),
    ]

    whole_members = whole_ring.members(tensor_at)
    seq_members = seq_ring.members(part_at)
    numbers = jnp.stack(
        [at * tok_rows for at in whole_members]
        + [(at * tensor_count + tensor_at) // 2 for at in owners.listed()]
        + [(owners.here + 1) % 2]
    )
    ids_from = tensor_count

    def from_place(table):
        return jnp.concatenate(
            [
                lax.dynamic_slice_in_dim(table, at * tok_rows, tok_rows, 0)
                for at in seq_members
            ]
        )

    tables = from_place(jnp.array(rope_tables(length, head_size)))
    seg_row = lax.dynamic_index_in_dim(segments, seq_at, 0, keepdims=False)
    marks = from_place(jnp.stack([seg_row, jnp.arange(length, dtype=jnp.int32)], axis=1))
    places = (marks[:, :1], marks[:, :1].T, marks[:, 1:], marks[:, 1:].T)
    gains = jnp.stack([query_gain, key_gain])

    query_proj, query_low, key_proj, key_low = project_call(
        normed_all, pair_mats, gains, tables, []
    )
    wave = after(wave, query_low)
    count = owners.chips - 1
    found["value"] = jnp.concatenate([found["value"], *wave[:count]], axis=0)
    found["out"] = jnp.concatenate([found["out"], *wave[count:]], axis=1)
    value_rest, out_rest = owners.cross((found["value"], found["out"]))
    full_mats = [*pair_mats, (found["value"], value_rest)]
    cot_steps.hop(query_low)
    value_low = value_call(normed_all, found["value"], value_rest, cot_steps.blocks[1:])
    out_full = jnp.concatenate([found["out"], out_rest], axis=1)
    far_down = [owners.along(after(own_down, wave), s) for s in chip_shifts]

    def place_of(ring, k):
        return {0: [0], ring.count // 2: [ring.count - 1]}.get(k, [2 * k - 1, 2 * k])

    far_both = []
    attended = [None] * part_count

    def branch_parts(k, tokens):
        parts, tokens = [], list(tokens)
        if k == 0:
            tokens += far_down
            far_both.extend(owners.along(after(own_both, *far_down), s) for s in chip_shifts)
        for b in place_of(seq_ring, k):
            attended[b] = attend_call(
                query_low,
                key_low,
                value_low,
                places,
                head_size,
                b * tok_rows,
                tok_rows,
                tokens,
            )
            parts.append(plain_dot(attended[b], out_full).astype(LOW))
        if k == 1:
            cot_steps.settle(parts)
            parts = after(parts, cot_steps.pair)
        return parts

    branch = seq_ring.scatter(branch_parts)
    cot_steps.pair = after(cot_steps.pair, branch)
    cot_steps.hop()
    residual = inputs + owners.unlist_columns(branch)
    inv_two = lax.rsqrt(jnp.mean(residual * residual, axis=-1, keepdims=True) + EPSILON)
    unit_two = residual * inv_two
    normed_two = (unit_two * mix_gain).astype(jnp.bfloat16)
    logits = jnp.dot(normed_two, w_router, preferred_element_type=jnp.float32)
    hits = jnp.any(
        routes[:, :, None] == jnp.arange(expert_count, dtype=jnp.int32)[None, None, :], axis=1
    )
    top_logit = jnp.max(jnp.where(hits, logits, MASKED), axis=-1, keepdims=True)
    raised = jnp.where(hits, jnp.exp(logits - top_logit), 0.0)
    gate_table = raised / jnp.sum(raised, axis=-1, keepdims=True)

    grad_out = cotangent.astype(jnp.float32)
    slab_mats = {0: [own_slab, both_slabs]}
    row_blocks, sums, mixed = ([None] * tensor_count for _ in range(3))
    shared_all = []

    def run_experts(shift, k, tokens):
        at = place_of(whole_ring, k)
        if len(shared_all) == shift:
            shared_all.append([None] * (2 if shift else 4))
        parts, mixed_parts, shared_all[shift] = experts_call(
            expert_count,
            numbers,
            [ids_from + shift, ids_from + owners.chips + shift],
            [None, None if shift else ids_from + owners.count],
            at,
            [row_blocks[b] for b in at],
            [cot_steps.blocks[b] for b in at],
            slab_mats[shift],
            [[part[b] for b in at] for part in (sums, mixed)] if shift else None,
            shared_all[shift],
            total_rows,
            tokens,
        )
        for b, part, mixed_part in zip(at, parts, mixed_parts):
            sums[b], mixed[b] = part, mixed_part
        return [sums[b] for b in at]

    def first_pair(k, blocks):
        for b, rows in zip(place_of(whole_ring, k), blocks):
            row_blocks[b] = rows
        run_experts(0, k, [])

    def next_hop(k, pair):
        done = [sums[b] for b in place_of(whole_ring, k - 1)]
        if k == 1:
            pair, cot_steps.pair = after((pair, cot_steps.pair), *done)
            while cot_steps.hops < tensor_count // 2:
                cot_steps.hop()
        elif k == 2:
            pair, cot_steps.pair = after((pair, cot_steps.pair), *done)
            cot_steps.settle()
            far_down[:] = after(far_down, pair)
            found["down"] = owners.cross(far_down)
        elif k == tensor_count // 2 - 1:
            pair, far_both[:], found["down"] = after((pair, far_both, found["down"]), *done)
        elif k < tensor_count // 2:
            pair = after(pair, *done)
        return pair

    high = lax.reduce_precision(gate_table, 8, 7)
    room = -2 * expert_count % 128
    payload = jnp.concatenate(
        [
            normed_two,
            high.astype(LOW),
            (gate_table - high).astype(LOW),
            jnp.zeros((tok_rows, room), LOW),
        ],
        axis=1,
    )
    whole_ring.gather(payload, first_pair, next_hop)
    far_other = owners.cross(far_both)
    for i, shift in enumerate(chip_shifts):
        slab_mats[shift] = [
            (far_both[i], far_both[i], far_down[i]),
            (far_other[i], far_other[i], found["down"][i]),
        ]
    for shift in range(1, owners.chips - 1):
        for k in range(tensor_count // 2 + 1):
            run_experts(shift, k, [])

    def last_pair(k, tokens):
        return run_experts(owners.chips - 1, k, jax.tree.leaves(tokens))

    def down_grads(shift, other, terms, tokens):
        kept, all_cot = shared_all[shift][0], shared_all[0][3]
        return slab_grads_call(all_cot, kept, other * hidden, hidden, False, terms, tokens)[0]

    def pre_grads(shift, other, terms, tokens):
        kept, rows = shared_all[shift][1], shared_all[0][2]
        return slab_grads_call(rows, kept, 2 * other * hidden, hidden, True, terms, tokens)[0]

    def finish(pair):
        others = [down_grads(s, 1, [], [sums[0]]) for s in chip_shifts]
        pair, others = after((pair, others))
        found["down"] = owners.cross(others)
        return pair

    summed_rows = whole_ring.scatter(last_pair, finish)
    grad_rows_sum = summed_rows[:, :model_width]
    grad_gates = summed_rows[:, model_width : model_width + expert_count]

    grad_logits = gate_table * (
        grad_gates - jnp.sum(gate_table * grad_gates, axis=-1, keepdims=True)
    )
    grad_normed_two = grad_rows_sum + outer_rows(grad_logits, w_router.astype(jnp.float32), HIGH)
    grad_router = inner_rows(grad_logits, normed_two.astype(jnp.float32), HIGH)
    grad_unit_two = grad_normed_two * mix_gain
    grad_mix_gain = jnp.sum(grad_normed_two * unit_two, axis=0)
    grad_residual = grad_out + inv_two * (
        grad_unit_two - unit_two * jnp.mean(grad_unit_two * unit_two, axis=-1, keepdims=True)
    )
    grad_branch = owners.list_columns(grad_residual.astype(jnp.bfloat16))
    gathered_back, sent_down = [], []
    mixture_steps = Reduction(whole_ring)

    def back_hop(k, pair):
        if k == 1:
            down = [
                down_grads(s, 0, [other], [grad_branch])
                for s, other in zip(chip_shifts, found["down"])
            ]
            sent_down.extend(owners.along(part, -s) for s, part in zip(chip_shifts, down))
            others = [pre_grads(s, 1, [], down) for s in chip_shifts]
            pair, others = after((pair, others))
            mixture_steps.hop(mixed[-1:], pair[0])
            others = [owners.cross(other) for other in others]
            found["pre"] = [
                pre_grads(s, 0, [other], [pair[0]]) for s, other in zip(chip_shifts, others)
            ]
            found["attn"] = attended_back_call(
                [*gathered_back, *pair], out_full, None, 0, length, found["pre"]
            )
        elif k == part_count // 2:
            pair, mixture_steps.pair = after((pair, mixture_steps.pair), found["attn"])
        return pair

    seq_ring.gather(grad_branch, lambda k, blocks: gathered_back.extend(blocks), back_hop)
    grad_attn = found["attn"]
    for b in range(3, part_count):
        grad_attn = attended_back_call(
            [gathered_back[b]], out_full, grad_attn, b * tok_rows, length, []
        )

    def mixture_hop(k, *tokens):
        mixture_steps.hop([mixed[b] for b in place_of(whole_ring, k)], *tokens)

    mixture_steps.pair, sent_down[:] = after((mixture_steps.pair, sent_down), grad_attn)
    mixture_hop(tensor_count // 2 - 1)
    sent_pre = [
        owners.along(part, -s) for s, part in zip(chip_shifts, found["pre"])
    ]
    *head_grads, grad_gains = attend_back_call(
        query_low,
        key_low,
        value_low,
        grad_attn,
        query_proj,
        key_proj,
        gains,
        tables,
        places,
        list(mixture_steps.sent),
    )

    own_other_half = weight_back_call(
        normed_all,
        gathered_back,
        head_grads,
        attended,
        1,
        list(mixture_steps.pair),
    )
    other_half = owners.cross(own_other_half)
    mine_half = weight_back_call(
        normed_all, gathered_back, head_grads, attended, 0, [own_other_half]
    )
    mixture_steps.pair = after(mixture_steps.pair, own_other_half)
    mixture_hop(max(tensor_count // 2 - 2, 1))
    normed_parts = rows_back_call(
        head_grads, full_mats, tok_rows, [mine_half, *mixture_steps.sent]
    )
    mixture_steps.pair = after(mixture_steps.pair, normed_parts[-1])
    for k in range(tensor_count // 2 - 3, 0, -1):
        mixture_hop(k)
    listed_norm = gain_call(
        own_other_half,
        mine_half,
        [m for pair in full_mats for m in pair],
        local_width,
        [*mixture_steps.sent, *sent_pre],
    )
    grad_norm_gain = owners.unlist_columns(listed_norm.T) / norm_gain
    room = model_width - grad_gains.size
    small_steps = Everywhere(
        jnp.concatenate(
            [
                grad_router,
                grad_mix_gain[None],
                grad_norm_gain,
                jnp.pad(grad_gains.reshape(1, -1), ((0, 0), (0, room))),
            ]
        )
    )
    small_steps.hop()
    chip_rows = model_width // owners.count
    piece_rows = chip_rows // 2
    pieces = [slice(p * piece_rows, (p + 1) * piece_rows) for p in range(2)]

    def both_cores(shift, rows, columns=slice(None)):
        rows = slice(shift * chip_rows + rows.start, shift * chip_rows + rows.stop)
        return mine_half[rows, columns].astype(FULL) + other_half[rows, columns].astype(FULL)

    sent_parts = [[both_cores(s, rows).astype(LOW) for s in chip_shifts] for rows in pieces]
    come = []

    def give_parts(k, tokens):
        parts = [normed_parts[b] for b in place_of(seq_ring, k)]
        if k == 1:
            parts, sent_parts[:], small_steps.value = after(
                (parts, sent_parts, small_steps.value)
            )
        if k == 0:
            sent = after(sent_parts[0], tokens)
            come.append([owners.along(part, -s) for s, part in zip(chip_shifts, sent)])
            found["own_other_down"] = down_grads(0, 1, [], tokens)
            found["own_other"] = pre_grads(0, 1, [], [found["own_other_down"]])
        return parts

    def normed_done(pair):
        pair, come[0], mixture_steps.pair = after(
            (pair, come[0], mixture_steps.pair), found["own_other"]
        )
        return pair

    grad_normed_one = seq_ring.scatter(give_parts, normed_done)
    done = grad_normed_one
    grad_normed_one = owners.unlist_columns(grad_normed_one)
    sent = after(sent_parts[1], done)
    come.append([owners.along(part, -s) for s, part in zip(chip_shifts, sent)])
    small_steps.value = after(small_steps.value, done)
    small_steps.hop()
    def columns_of(place, seq):
        first = (place * seq_count + seq) * block_width
        return slice(first, first + block_width)

    def summed_piece(p, columns):
        return both_cores(0, pieces[p], columns) + sum(
            part[:, columns].astype(FULL) for part in come[p]
        )

    def swap_piece(p):
        return [
            seq_swap(
                jnp.concatenate(
                    [summed_piece(p, columns_of(place, s)).astype(LOW) for place in range(4)],
                    axis=1,
                ),
                -s,
            )
            for s in seq_shifts
        ]

    own_other_down, own_other = owners.cross(
        after((found["own_other_down"], found["own_other"]), done)
    )
    (grad_down,) = slab_grads_call(
        shared_all[0][3],
        shared_all[0][0],
        0,
        hidden,
        False,
        [own_other_down, *sent_down],
        [done],
        kind=FULL,
    )
    swapped_pieces = [swap_piece(0)]
    come[1], small_steps.value, swapped_pieces[0] = after(
        (come[1], small_steps.value, swapped_pieces[0]), grad_down
    )
    small_steps.hop()
    grad_gate, grad_up = slab_grads_call(
        shared_all[0][2],
        shared_all[0][1],
        0,
        hidden,
        True,
        [own_other, *sent_pre],
        come[1],
        parts=2,
        kind=FULL,
    )
    swapped_pieces.append(swap_piece(1))
    small_steps.value = after(small_steps.value, grad_gate)
    layer_out = (residual + mixture_steps.total(mixed[0])).astype(jnp.bfloat16)
    grad_unit_one = grad_normed_one * norm_gain
    grad_tokens = grad_residual + inv_one * (
        grad_unit_one - unit_one * jnp.mean(grad_unit_one * unit_one, axis=-1, keepdims=True)
    )
    grad_tokens = grad_tokens.astype(jnp.bfloat16)
    swapped_pieces = after(swapped_pieces, layer_out, grad_tokens, grad_gate)
    owned = [[] for _ in range(4)]
    for p, swapped in enumerate(swapped_pieces):
        for place in range(4):
            columns = slice(place * block_width, (place + 1) * block_width)
            owned[place].append(
                summed_piece(p, columns_of(place, 0))
                + sum(part[:, columns].astype(FULL) for part in swapped)
            )
    owned_query, owned_key, owned_value, owned_out = map(jnp.concatenate, owned)
    owned_out = owned_out.T
    while small_steps.value is not None:
        small_steps.hop()
    small = small_steps.own
    small_gains = small[-1, : grad_gains.size].reshape(grad_gains.shape)
    return (
        layer_out,
        grad_tokens,
        small[-2],
        owned_query,
        owned_key,
        owned_value,
        small_gains[0],
        small_gains[1],
        owned_out,
        small[-3],
        small[:-3].T,
        grad_gate[None],
        grad_up[None],
        grad_down[None],
    )


def solution(mesh):
    in_specs = (
        P(("expert", "tensor"), None),
        P("expert", None),
        P(("expert", "tensor"), None),
        P(),
        P("expert", "tensor"),
        P("expert", "tensor"),
        P("expert", "tensor"),
        P(),
        P(),
        P("tensor", "expert"),
        P(),
        P(),
        P(("expert", "tensor"), None, None),
        P(("expert", "tensor"), None, None),
        P(("expert", "tensor"), None, None),
        P(("expert", "tensor"), None),
    )
    out_specs = (
        P(("expert", "tensor"), None),
        P(("expert", "tensor"), None),
        P(),
        P("expert", "tensor"),
        P("expert", "tensor"),
        P("expert", "tensor"),
        P(),
        P(),
        P("tensor", "expert"),
        P(),
        P(),
        P(("expert", "tensor"), None, None),
        P(("expert", "tensor"), None, None),
        P(("expert", "tensor"), None, None),
    )
    return jax.shard_map(
        per_device, mesh=mesh, in_specs=in_specs, out_specs=out_specs, check_vma=False
    )
```
